256 devices in a mesh: row: 8 (over x, y_hi), col: 32 (over z, y_lo, core).
Axes of the slice: x: 4, y: 4 (y_hi: 2, y_lo: 2; y = y_hi * 2 + y_lo), z: 8, core: 2. Of those that a mesh axis runs over, the one named last changes fastest.
Arguments:
- density: bfloat16 [8192, 8192], P('row', 'col'), as said below
- pattern: int32 [64, 64], replicated, may hold values from 0 to 1, as said below
Outputs:
- square: bfloat16 [8192, 8192], P('row', 'col')
- traces: float32 [2], replicated
The draws below stay inside these ranges and needn't reach their ends.
Inputs may be any that keep to these rules, and one draw needn't show every extreme that they name: Every diagonal block of 128 x 128 entries of density is symmetric. `pattern`: block (0, 63) is always stored.
All inputs are finite; a program needn't handle non-finite values.
Results may differ from the reference program's by a relative error of at most 0.0013.
Values may be sent and summed in bfloat16 or wider, within the bound.
A program may use at most 64 MiB of HBM per device.

```python
import math
import jax
import jax.numpy as jnp

BLK = 128
NB = 64
N = 8192


def draw_density(key, part):
    key_off, key_diag = jax.random.split(jax.random.fold_in(key, 11), 2)
    base = jax.random.normal(key_off, (N, N), jnp.float32)
    index_ids = jnp.arange(N)
    block_ids = index_ids // BLK
    same_block = block_ids[:, None] == block_ids[None, :]
    sym_part = (base + base.T) * math.sqrt(0.5)
    entries = jnp.where(same_block, sym_part, base) * math.sqrt(2.0 / N)
    on_diag = index_ids[:, None] == index_ids[None, :]
    scaled = entries
    diag_vals = jax.random.uniform(key_diag, (N,), jnp.float32, 0.1, 0.9)
    result = jnp.where(on_diag, diag_vals[:, None] * jnp.ones((1, N), jnp.float32), scaled)
    return result.astype(jnp.bfloat16)


def draw_pattern(key, part):
    key = jax.random.fold_in(key, 23)
    values = jax.random.randint(key, (NB, NB), 0, 2).astype(jnp.int32)
    return values.at[0, NB - 1].set(1)


def setup_inputs(seed: int = 0) -> dict:
    keys = jax.random.split(jax.random.key(seed), 3)
    density = draw_density(jax.random.fold_in(keys[2], 71), 0)
    pattern = draw_pattern(jax.random.fold_in(keys[2], 71), 0)
    return {"density": density, "pattern": pattern}


def expand(block_mask):
    return jnp.repeat(jnp.repeat(block_mask, BLK, axis=0), BLK, axis=1)


def reference(density, pattern):
    block_ids = jnp.arange(NB)
    diagonal_blk = block_ids[:, None] == block_ids[None, :]
    above = block_ids[None, :] >= block_ids[:, None]
    kept_blocks = ((pattern != 0) | diagonal_blk) & above
    strict_blocks = kept_blocks & jnp.logical_not(diagonal_blk)
    zeros_like = jnp.zeros_like(density)
    stored = jnp.where(expand(kept_blocks), density, zeros_like)
    lower_part = jnp.where(expand(strict_blocks), density, zeros_like).T
    full_matrix = stored + lower_part
    product = jnp.dot(full_matrix, full_matrix, preferred_element_type=jnp.float32)
    trace_first = jnp.sum(jnp.diagonal(full_matrix).astype(jnp.float32))
    trace_second = jnp.sum(jnp.diagonal(product))
    square = jnp.where(expand(kept_blocks), product, jnp.zeros_like(product)).astype(jnp.bfloat16)
    traces = jnp.stack([trace_first, trace_second]) / N
    return square, traces
```

```python
import jax
import jax.numpy as jnp
from jax import lax
from jax.experimental import pallas as pl
from jax.experimental.pallas import tpu as pltpu
from jax.sharding import PartitionSpec as P

BLK = 128
MESH = pl.DeviceIdType.MESH
TILE = 256
SUPER = 1024
NSUP = 8
CHUNKS = 4


def ring_order(r, p):
    x, hi = lax.div(r, 2), lax.rem(r, 2)
    xx = lax.rem(x + 2 * p, 4)
    return xx * (1 - hi) + (7 - xx) * hi


def ring_row(h, p):
    hi = lax.div(h, 4)
    xx = h * (1 - hi) + (7 - h) * hi
    return 2 * lax.rem(xx + 2 * p, 4) + hi


def kernel(
    pat, dens, out,
    tbuf, ttbuf, rowb, colb, part, sibb, ysend, yrecv,
    ring_s, ring_r, intra_s, intra_r, mirr_s, mirr_r, mirc_s, mirc_r,
    sib_s, sib_r, y_s, y_r,
):
    r = lax.axis_index("row")
    c = lax.axis_index("col")
    z, s = lax.div(c, 4), lax.rem(c, 4)
    p, q = lax.div(s, 2), lax.rem(s, 2)
    upper, diag, lower = r < z, r == z, r > z

    def dev(r_, z_, s_):
        return (r_, 4 * z_ + s_)

    def copy(src, dst, ssem, rsem, device):
        return pltpu.make_async_remote_copy(
            src_ref=src, dst_ref=dst, send_sem=ssem, recv_sem=rsem,
            device_id=device, device_id_type=MESH,
        )

    h = ring_order(r, p)
    z_next, z_prev = lax.rem(z + 1, 8), lax.rem(z + 7, 8)
    r_next, r_prev = ring_row(lax.rem(h + 1, 8), p), ring_row(lax.rem(h + 7, 8), p)
    neighbours = (
        (dev(r, z_next, s), dev(r, z_prev, s)),
        (dev(r_next, z, s), dev(r_prev, z, s)),
    )
    others = [lax.rem(s + d, 4) for d in (1, 2, 3)]

    barrier = pltpu.get_barrier_semaphore()
    for ring in neighbours:
        for device in ring:
            pl.semaphore_signal(barrier, inc=1, device_id=device, device_id_type=MESH)
    for o in others:
        pl.semaphore_signal(barrier, inc=1, device_id=dev(r, z, o), device_id_type=MESH)

    @pl.when(r != z)
    def _():
        for o in range(4):
            pl.semaphore_signal(barrier, inc=1, device_id=dev(z, r, o), device_id_type=MESH)

    def keep(i, j):
        bi, bj = r * 8 + i, c * 2 + j
        return ((pat[bi, bj] != 0) | (bi == bj)) & (bj >= bi), bi == bj

    for i in range(8):
        for j in range(2):
            kept, same = keep(i, j)
            block = dens[pl.ds(i * BLK, BLK), pl.ds(j * BLK, BLK)].astype(jnp.float32)
            block = jnp.where(kept, block, jnp.zeros_like(block))
            tbuf[pl.ds(i * BLK, BLK), pl.ds(j * BLK, BLK)] = block.astype(jnp.bfloat16)
            strict = jnp.where(same, jnp.zeros_like(block), block)
            ttbuf[pl.ds(j * BLK, BLK), pl.ds(i * BLK, BLK)] = strict.T.astype(jnp.bfloat16)

    pl.semaphore_wait(barrier, 7 + 4 * (r != z).astype(jnp.int32))

    def quarter(i):
        return pl.ds(pl.multiple_of(i * TILE, TILE), TILE)

    def row_slot(k):
        return rowb.at[:, quarter(k)]

    def col_slot(k):
        return colb.at[quarter(k), :]

    def intra(o):
        return copy(
            tbuf.at[quarter(o), :], colb.at[quarter(r), quarter(s)],
            intra_s.at[o], intra_r.at[s], dev(r, z, o),
        )

    def intra_in(o):
        return copy(
            tbuf.at[quarter(o), :], colb.at[quarter(r), quarter(o)],
            intra_s.at[o], intra_r.at[o], dev(r, z, o),
        )

    def mirror_row(o):
        return copy(
            ttbuf.at[:, quarter(o)], rowb.at[quarter(s), quarter(r)],
            mirr_s.at[o], mirr_r.at[s], dev(z, r, o),
        )

    def mirror_row_in(o):
        return copy(
            ttbuf.at[:, quarter(o)], rowb.at[quarter(o), quarter(z)],
            mirr_s.at[o], mirr_r.at[o], dev(z, r, o),
        )

    def mirror_col(slot):
        return copy(ttbuf, col_slot(slot), mirc_s, mirc_r, dev(z, r, s))

    @pl.when(upper)
    def _():
        mirror_col(z).start()
        for o in range(4):
            mirror_row(o).start()
        for o in others:
            intra(o).start()
        rowb[:, quarter(z)] = tbuf[...]
        colb[quarter(r), quarter(s)] = tbuf[quarter(s), :]
        for o in others:
            intra_in(o).wait_recv()

    @pl.when(diag)
    def _():
        for o in others:
            mirror_row(o).start()
        for o in others:
            intra(o).start()
        rowb[quarter(s), quarter(z)] = ttbuf[:, quarter(s)]
        colb[quarter(r), quarter(s)] = tbuf[quarter(s), :]
        for o in others:
            mirror_row_in(o).wait_recv()
            intra_in(o).wait_recv()
        rowb[:, quarter(z)] = rowb[:, quarter(z)] + tbuf[...]
        colb[quarter(r), :] = colb[quarter(r), :] + ttbuf[...]

    @pl.when(lower)
    def _():
        mirror_col(r).wait_recv()
        for o in range(4):
            mirror_row_in(o).wait_recv()

    away, home = (1 - p) * 2, p * 2

    def col_quarter(ch):
        return (away if ch < 2 else home) + ch % 2

    def ring_copy(ring, d, ch, item):
        t_sem = item[1]
        k = item[0]
        if ring == 0:
            ref = rowb.at[pl.ds(ch * TILE, TILE), quarter(k)]
        else:
            ref = colb.at[quarter(k), quarter(col_quarter(ch))]
        return copy(
            ref, ref, ring_s.at[ring, d, ch, t_sem - 1], ring_r.at[ring, d, ch, t_sem - 1],
            neighbours[ring][d],
        )

    def item_at(ring, d, dist):
        pos = z if ring == 0 else h
        pos = lax.rem(pos + (8 - dist if d == 0 else dist), 8)
        return pos if ring == 0 else ring_row(pos, p)

    def is_sent(d, ch, t):
        return t <= 3 or ch % 2 == d

    def send(ring, d, ch, t):
        return ring_copy(ring, d, ch, (item_at(ring, d, t - 1), t))

    def recv(ring, d, ch, t):
        return ring_copy(ring, d, ch, (item_at(ring, d, t), t))

    ringdirs = [(a, d) for a in range(2) for d in range(2)]

    def step(ch, t):
        for a, d in ringdirs:
            if not is_sent(d, ch, t):
                continue
            if t > 1:
                recv(a, d, ch, t - 1).wait_recv()
            send(a, d, ch, t).start()

    def drain(ch):
        for a, d in ringdirs:
            if is_sent(d, ch, 4):
                recv(a, d, ch, 4).wait_recv()
            else:
                recv(a, d, ch, 3).wait_recv()

    def pair_round(c0, c1, extra):
        for t in (2, 3, 4):
            step(c0, t)
            step(c1, t)
        for e in extra:
            step(e, 1)
        drain(c0)
        drain(c1)

    def matmul(m0, nq):
        cols = quarter(nq)

        def body(i, carry):
            rows = pl.ds(pl.multiple_of(m0 + i * TILE, TILE), TILE)
            part[rows, cols] = jnp.dot(
                rowb[rows, :], colb[:, cols], preferred_element_type=jnp.float32
            )
            return carry

        lax.fori_loop(0, 2, body, 0)

    sibling = dev(r, z, lax.rem(s, 2) * 0 + 2 * p + (1 - q))
    partner = dev(r, z, 2 * (1 - p) + q)
    half = SUPER // 2

    def sib_away(i):
        rows = pl.ds(i * half, half)
        return copy(
            part.at[rows, quarter(away + 1 - q)], sibb.at[rows, pl.ds(0, TILE)],
            sib_s.at[i], sib_r.at[i], sibling,
        )

    def sib_home():
        return copy(
            part.at[:, quarter(home + 1 - q)], sibb.at[:, pl.ds(TILE, TILE)],
            sib_s.at[2], sib_r.at[2], sibling,
        )

    def y_copy(i):
        rows = pl.ds(i * half, half)
        return copy(ysend.at[rows, :], yrecv.at[rows, :], y_s.at[i], y_r.at[i], partner)

    def away_part(i):
        matmul(i * half, away + 1 - q)
        sib_away(i).start()
        matmul(i * half, away + q)
        sib_away(i).wait_recv()
        rows = pl.ds(i * half, half)
        ysend[rows, :] = part[rows, quarter(away + q)] + sibb[rows, pl.ds(0, TILE)]
        y_copy(i).start()

    step(0, 1)
    step(1, 1)
    pair_round(0, 1, (2, 3))
    away_part(0)
    pair_round(2, 3, ())
    away_part(1)
    for i in range(2):
        matmul(i * half, home + 1 - q)
    sib_home().start()
    for i in range(2):
        matmul(i * half, home + q)
    sib_home().wait_recv()
    for i in range(2):
        y_copy(i).wait_recv()
    for i in range(8):
        rows = pl.ds(i * BLK, BLK)
        value = part[rows, quarter(home + q)] + sibb[rows, pl.ds(TILE, TILE)] + yrecv[rows, :]
        for j in range(2):
            kept, _same = keep(i, j)
            block = value[:, j * BLK:(j + 1) * BLK]
            block = jnp.where(kept, block, jnp.zeros_like(block))
            out[rows, pl.ds(j * BLK, BLK)] = block.astype(jnp.bfloat16)

    for ch in range(CHUNKS):
        for t in (1, 2, 3, 4):
            for a, d in ringdirs:
                if is_sent(d, ch, t):
                    send(a, d, ch, t).wait_send()
    for i in range(2):
        sib_away(i).wait_send()
        y_copy(i).wait_send()
    sib_home().wait_send()

    @pl.when(upper)
    def _():
        mirror_col(z).wait_send()
        for o in range(4):
            mirror_row(o).wait_send()
        for o in others:
            intra(o).wait_send()

    @pl.when(diag)
    def _():
        for o in others:
            mirror_row(o).wait_send()
            intra(o).wait_send()


def square_tile(pattern, density):
    dma = pltpu.SemaphoreType.DMA
    return pl.pallas_call(
        kernel,
        out_shape=jax.ShapeDtypeStruct(density.shape, jnp.bfloat16),
        in_specs=[
            pl.BlockSpec(memory_space=pltpu.SMEM),
            pl.BlockSpec(memory_space=pltpu.VMEM),
        ],
        out_specs=pl.BlockSpec(memory_space=pltpu.VMEM),
        scratch_shapes=[
            pltpu.VMEM((SUPER, TILE), jnp.bfloat16),
            pltpu.VMEM((TILE, SUPER), jnp.bfloat16),
            pltpu.VMEM((SUPER, NSUP * TILE), jnp.bfloat16),
            pltpu.VMEM((NSUP * TILE, SUPER), jnp.bfloat16),
            pltpu.VMEM((SUPER, SUPER), jnp.float32),
            pltpu.VMEM((SUPER, 2 * TILE), jnp.float32),
            pltpu.VMEM((SUPER, TILE), jnp.float32),
            pltpu.VMEM((SUPER, TILE), jnp.float32),
            dma((2, 2, CHUNKS, 4)), dma((2, 2, CHUNKS, 4)),
            dma((4,)), dma((4,)), dma((4,)), dma((4,)), dma, dma,
            dma((3,)), dma((3,)), dma((2,)), dma((2,)),
        ],
        compiler_params=pltpu.CompilerParams(
            collective_id=0, has_side_effects=True, vmem_limit_bytes=40 * 1024 * 1024
        ),
        cost_estimate=pl.CostEstimate(
            flops=2 * SUPER * SUPER * NSUP * TILE, bytes_accessed=16 * 1024 * 1024, transcendentals=0
        ),
    )(pattern, density)


def per_device(density, pattern):
    n_row, n_col = lax.axis_size("row"), lax.axis_size("col")
    row_index, col_index = lax.axis_index("row"), lax.axis_index("col")
    height, width = density.shape
    row_blocks, col_blocks = height // BLK, width // BLK
    block_rows = row_index * row_blocks + jnp.arange(row_blocks)[:, None]
    block_cols = col_index * col_blocks + jnp.arange(col_blocks)[None, :]
    chosen = lax.dynamic_slice(
        pattern, (row_index * row_blocks, col_index * col_blocks), (row_blocks, col_blocks)
    )
    same = block_rows == block_cols
    kept = ((chosen != 0) | same) & (block_cols >= block_rows)
    weight = jnp.where(same, 1.0, jnp.where(kept, 2.0, 0.0)).astype(jnp.float32)
    values = density.astype(jnp.float32)
    rows = row_index * height + lax.broadcasted_iota(jnp.int32, density.shape, 0)
    cols = col_index * width + lax.broadcasted_iota(jnp.int32, density.shape, 1)
    first = jnp.sum(jnp.where(rows == cols, values, 0.0))
    squares = jnp.where(values == 0.0, 0.0, values * values)
    by_block = squares.reshape(row_blocks, BLK, width).sum(axis=1)
    by_block = by_block.reshape(row_blocks, col_blocks, BLK).sum(axis=2)
    second = jnp.sum(jnp.where(kept, weight * by_block, 0.0))
    sums = lax.psum(jnp.stack([first, second]), ("row", "col"))
    square = square_tile(pattern, density)
    return square, sums / (height * n_row)


def solution(mesh):
    return jax.shard_map(
        per_device, mesh=mesh, in_specs=(P("row", "col"), P()),
        out_specs=(P("row", "col"), P()), check_vma=False,
    )
```

```python
import jax
import jax.numpy as jnp
from jax import lax
from jax.experimental import pallas as pl
from jax.experimental.pallas import tpu as pltpu
from jax.sharding import PartitionSpec as P

BLK = 128
MESH = pl.DeviceIdType.MESH
TILE = 256
SUPER = 1024
NSUP = 8
CHUNKS = 4


def ring_order(r, p):
    x, hi = lax.div(r, 2), lax.rem(r, 2)
    xx = lax.rem(x + 2 * p, 4)
    return xx * (1 - hi) + (7 - xx) * hi


def ring_row(h, p):
    hi = lax.div(h, 4)
    xx = h * (1 - hi) + (7 - h) * hi
    return 2 * lax.rem(xx + 2 * p, 4) + hi


def kernel(
    pat, dens, out, traces,
    tbuf, ttbuf, rowb, colb, part, sibb, ysend, yrecv, tr, trq,
    ring_s, ring_r, inj_s, inj_r, tr_s, tr_r, trq_s, trq_r,
    intra_s, intra_r, mirr_s, mirr_r, sib_s, sib_r, y_s, y_r,
):
    r = lax.axis_index("row")
    c = lax.axis_index("col")
    z, s = lax.div(c, 4), lax.rem(c, 4)
    p, q = lax.div(s, 2), lax.rem(s, 2)
    active, diag = r <= z, r == z

    def dev(r_, z_, s_):
        return (r_, 4 * z_ + s_)

    def copy(src, dst, ssem, rsem, device):
        return pltpu.make_async_remote_copy(
            src_ref=src, dst_ref=dst, send_sem=ssem, recv_sem=rsem,
            device_id=device, device_id_type=MESH,
        )

    def wrap(i):
        return lax.rem(i + 8, 8)

    h = ring_order(r, p)
    neighbours = (
        (dev(r, wrap(z + 1), s), dev(r, wrap(z - 1), s)),
        (dev(ring_row(wrap(h + 1), p), z, s), dev(ring_row(wrap(h - 1), p), z, s)),
    )
    others = [lax.rem(s + d, 4) for d in (1, 2, 3)]

    barrier = pltpu.get_barrier_semaphore()
    for ring in neighbours:
        for device in ring:
            pl.semaphore_signal(barrier, inc=1, device_id=device, device_id_type=MESH)
    for o in others:
        pl.semaphore_signal(barrier, inc=1, device_id=dev(r, z, o), device_id_type=MESH)

    def keep(i, j):
        bi, bj = r * 8 + i, c * 2 + j
        return ((pat[bi, bj] != 0) | (bi == bj)) & (bj >= bi), bi == bj

    def quarter(i):
        return pl.ds(pl.multiple_of(i * TILE, TILE), TILE)

    eye = lax.broadcasted_iota(jnp.int32, (BLK, BLK), 0) == lax.broadcasted_iota(jnp.int32, (BLK, BLK), 1)
    first = jnp.zeros((BLK, BLK), jnp.float32)
    second = jnp.zeros((BLK, BLK), jnp.float32)
    for i in range(8):
        for j in range(2):
            kept, same = keep(i, j)
            block = dens[pl.ds(i * BLK, BLK), pl.ds(j * BLK, BLK)].astype(jnp.float32)
            block = jnp.where(kept, block, jnp.zeros_like(block))
            tbuf[pl.ds(i * BLK, BLK), pl.ds(j * BLK, BLK)] = block.astype(jnp.bfloat16)
            first = first + jnp.where(eye & same, block, jnp.zeros_like(block))
            square = block * block
            second = second + jnp.where(same, square, square + square)

            @pl.when(diag)
            def _():
                strict = jnp.where(same, jnp.zeros_like(block), block)
                ttbuf[pl.ds(j * BLK, BLK), pl.ds(i * BLK, BLK)] = strict.T.astype(jnp.bfloat16)

    tr[0, z, 0:8, :] = first.reshape(BLK // 8, 8, BLK).sum(axis=0)
    tr[0, z, 8:16, :] = second.reshape(BLK // 8, 8, BLK).sum(axis=0)

    pl.semaphore_wait(barrier, 7)

    def intra(o):
        return copy(
            tbuf.at[quarter(o), :], colb.at[quarter(r), quarter(s)],
            intra_s.at[o], intra_r.at[s], dev(r, z, o),
        )

    def intra_in(o):
        return copy(
            tbuf.at[quarter(o), :], colb.at[quarter(r), quarter(o)],
            intra_s.at[o], intra_r.at[o], dev(r, z, o),
        )

    def mirror(o):
        return copy(
            ttbuf.at[:, quarter(o)], rowb.at[quarter(s), quarter(z)],
            mirr_s.at[o], mirr_r.at[s], dev(r, z, o),
        )

    def mirror_in(o):
        return copy(
            ttbuf.at[:, quarter(o)], rowb.at[quarter(o), quarter(z)],
            mirr_s.at[o], mirr_r.at[o], dev(r, z, o),
        )

    away, home = (1 - p) * 2, p * 2
    center = (r, ring_order(z, p))
    pos = (z, h)

    def chunk(ch):
        return quarter((away if ch < 2 else home) + ch % 2)

    def piece(ring, ch, k):
        return rowb.at[chunk(ch), quarter(k)] if ring == 0 else colb.at[quarter(k), chunk(ch)]

    def at(ring, where):
        return wrap(where) if ring == 0 else ring_row(wrap(where), p)

    def item_at(ring, d, dist):
        return at(ring, pos[ring] - dist if d == 0 else pos[ring] + dist)

    def stored(ring, k):
        return k >= r if ring == 0 else k <= z

    def has_hop(d, ch, t):
        return t <= 3 or (t == 4 and ch % 2 == d)

    def hop(ring, d, ch, t, k):
        ref = piece(ring, ch, k)
        return copy(
            ref, ref, ring_s.at[ring, d, ch, t - 1], ring_r.at[ring, d, ch, t - 1],
            neighbours[ring][d],
        )

    ringdirs = [(a, d) for a in range(2) for d in range(2)]

    def tr_hop(ring, d, t, k):
        ref = tr.at[ring, k]
        return copy(ref, ref, tr_s.at[ring, d, t - 1], tr_r.at[ring, d, t - 1], neighbours[ring][d])

    def own(ring, chs):
        @pl.when(active)
        def _():
            for ch in chs:
                for d in range(2):
                    hop(ring, d, ch, 1, item_at(ring, d, 0)).start()

    def tr_own(ring):
        for d in range(2):
            tr_hop(ring, d, 1, item_at(ring, d, 0)).start()

    def natural(chs, t):
        for ch in chs:
            for ring, d in ringdirs:
                if not has_hop(d, ch, t):
                    continue
                k = item_at(ring, d, t)

                @pl.when(stored(ring, k))
                def _():
                    hop(ring, d, ch, t, k).wait_recv()
                    if has_hop(d, ch, t + 1):
                        hop(ring, d, ch, t + 1, k).start()

    def tr_step(ring, t):
        for d in range(2):
            if has_hop(d, 0, t):
                k = item_at(ring, d, t)
                tr_hop(ring, d, t, k).wait_recv()
                if has_hop(d, 0, t + 1):
                    tr_hop(ring, d, t + 1, k).start()

    def mirrored(ring, e, d):
        source = (ring_order(r, p), z)[ring]
        k = at(1 - ring, source - d if e == 0 else source + d)
        return k, (k < r if ring == 0 else k > z)

    def along(ring, ch):
        return wrap(pos[ring] - center[ring] if ch % 2 == 0 else center[ring] - pos[ring])

    def last(ring, ch):
        if ring == 1:
            return jnp.where(z > 0, 7, 0)
        return 7 - r if ch % 2 == 0 else jnp.where(r < 7, 7, 0)

    def inj_hop(ring, e, d, ch, k):
        ref = piece(ring, ch, k)
        return copy(
            ref, ref, inj_s.at[ring, e, d - 1, ch], inj_r.at[ring, e, d - 1, ch],
            neighbours[ring][ch % 2],
        )

    def inject(chs, t):
        for ch in chs:
            for ring in range(2):
                j = along(ring, ch)
                end = last(ring, ch)
                d = t - j
                for e in range(2):
                    k, exists = mirrored(ring, e, d)
                    here = exists & (d >= 1) & (d <= (3 if e else 4)) & (j <= end)

                    @pl.when(here & (j > 0))
                    def _():
                        inj_hop(ring, e, d, ch, k).wait_recv()

                    if t <= 4:

                        @pl.when(here & (j == 0))
                        def _():
                            if ring == 0:
                                rowb[chunk(ch), quarter(k)] = colb[quarter(k), chunk(ch)].T
                            else:
                                colb[quarter(k), chunk(ch)] = rowb[chunk(ch), quarter(k)].T

                    @pl.when(here & (j < end))
                    def _():
                        inj_hop(ring, e, d, ch, k).start()

    def step(chs, t):
        if t <= 4:
            natural(chs, t)
        inject(chs, t)

    def matmul(m0, nq):
        cols = quarter(nq)

        def body(i, carry):
            rows = pl.ds(pl.multiple_of(m0 + i * TILE, TILE), TILE)
            part[rows, cols] = jnp.dot(
                rowb[rows, :], colb[:, cols], preferred_element_type=jnp.float32
            )
            return carry

        lax.fori_loop(0, 2, body, 0)

    sibling = dev(r, z, 2 * p + (1 - q))
    partner = dev(r, z, 2 * (1 - p) + q)
    half = SUPER // 2
    starts = (away * TILE, home * TILE)

    def rows_of(i):
        return pl.ds(pl.multiple_of(starts[i], half), half)

    def sib_away(i):
        rows = rows_of(i)
        return copy(
            part.at[rows, quarter(away + 1 - q)], sibb.at[rows, pl.ds(0, TILE)],
            sib_s.at[i], sib_r.at[i], sibling,
        )

    def sib_home():
        return copy(
            part.at[:, quarter(home + 1 - q)], sibb.at[:, pl.ds(TILE, TILE)],
            sib_s.at[2], sib_r.at[2], sibling,
        )

    def y_copy(i):
        rows = rows_of(i)
        return copy(ysend.at[rows, :], yrecv.at[rows, :], y_s.at[i], y_r.at[i], partner)

    def y_in(i):
        rows = rows_of(1 - i)
        return copy(ysend.at[rows, :], yrecv.at[rows, :], y_s.at[i], y_r.at[i], partner)

    def away_1(i):
        @pl.when(active)
        def _():
            matmul(starts[i], away + 1 - q)
            sib_away(i).start()

    def away_2(i):
        @pl.when(active)
        def _():
            matmul(starts[i], away + q)

    def away_3(i):
        @pl.when(active)
        def _():
            sib_away(i).wait_recv()
            rows = rows_of(i)
            ysend[rows, :] = part[rows, quarter(away + q)] + sibb[rows, pl.ds(0, TILE)]
            y_copy(i).start()

    def trq_copy(o):
        return copy(trq.at[s], trq.at[s], trq_s.at[o], trq_r.at[s], dev(r, z, o))

    def trq_in(o):
        return copy(trq.at[o], trq.at[o], trq_s.at[o], trq_r.at[o], dev(r, z, o))

    def total(ref, n):
        value = ref[0]
        for i in range(1, n):
            value = value + ref[i]
        return value

    @pl.when(active)
    def _():
        for o in others:
            intra(o).start()

    @pl.when(r < z)
    def _():
        rowb[:, quarter(z)] = tbuf[...]
        colb[quarter(r), quarter(s)] = tbuf[quarter(s), :]
        for o in others:
            intra_in(o).wait_recv()

    @pl.when(diag)
    def _():
        for o in others:
            mirror(o).start()
        rowb[quarter(s), quarter(z)] = ttbuf[:, quarter(s)]
        colb[quarter(r), quarter(s)] = tbuf[quarter(s), :]
        for o in others:
            mirror_in(o).wait_recv()
            intra_in(o).wait_recv()
        rowb[:, quarter(z)] = rowb[:, quarter(z)] + tbuf[...]
        colb[quarter(r), :] = colb[quarter(r), :] + ttbuf[...]

    tr_own(0)
    for ring in range(2):
        own(ring, (0, 1))
    for u in range(1, 16):
        if u == 3:
            for ring in range(2):
                own(ring, (2, 3))
        if u <= 11:
            step((0, 1), u)
        if u <= 4:
            tr_step(0, u)
        if u >= 5:
            step((2, 3), u - 4)
        if u == 5:
            tr[1, r] = total(tr.at[0], 8)
            tr_own(1)
        if 6 <= u <= 9:
            tr_step(1, u - 5)
        if u == 10:
            trq[s] = total(tr.at[1], 8)
            for o in others:
                trq_copy(o).start()
        if u == 12:
            away_1(0)
        if u == 13:
            away_2(0)
        if u == 14:
            away_3(0)
    away_1(1)
    away_2(1)
    away_3(1)

    @pl.when(active)
    def _():
        for i in range(2):
            matmul(i * half, home + 1 - q)
        sib_home().start()
        for i in range(2):
            matmul(i * half, home + q)

    for o in others:
        trq_in(o).wait_recv()
    sums = total(trq, 4)
    traces[0] = jnp.sum(sums[0:8, :]) / (NSUP * SUPER)
    traces[1] = jnp.sum(sums[8:16, :]) / (NSUP * SUPER)

    @pl.when(active)
    def _():
        sib_home().wait_recv()
        for i in range(2):
            y_in(i).wait_recv()
        for i in range(8):
            rows = pl.ds(i * BLK, BLK)
            value = part[rows, quarter(home + q)] + sibb[rows, pl.ds(TILE, TILE)] + yrecv[rows, :]
            for j in range(2):
                kept, _same = keep(i, j)
                block = value[:, j * BLK:(j + 1) * BLK]
                block = jnp.where(kept, block, jnp.zeros_like(block))
                out[rows, pl.ds(j * BLK, BLK)] = block.astype(jnp.bfloat16)

    @pl.when(r > z)
    def _():
        out[...] = jnp.zeros_like(out)

    for ring, d in ringdirs:
        for t in (1, 2, 3, 4):
            k = item_at(ring, d, t - 1)
            if has_hop(d, 0, t):
                tr_hop(ring, d, t, k).wait_send()

            @pl.when(stored(ring, k))
            def _():
                for ch in range(CHUNKS):
                    if has_hop(d, ch, t):
                        hop(ring, d, ch, t, k).wait_send()

    for ch in range(CHUNKS):
        for ring in range(2):
            for e in range(2):
                for d in range(1, 4 if e else 5):
                    k, exists = mirrored(ring, e, d)

                    @pl.when(exists & (along(ring, ch) < last(ring, ch)))
                    def _():
                        inj_hop(ring, e, d, ch, k).wait_send()

    for o in others:
        trq_copy(o).wait_send()

    @pl.when(active)
    def _():
        for i in range(2):
            sib_away(i).wait_send()
            y_copy(i).wait_send()
        sib_home().wait_send()
        for o in others:
            intra(o).wait_send()

    @pl.when(diag)
    def _():
        for o in others:
            mirror(o).wait_send()


def per_device(density, pattern):
    dma = pltpu.SemaphoreType.DMA
    f32, bf16 = jnp.float32, jnp.bfloat16
    return pl.pallas_call(
        kernel,
        out_shape=(
            jax.ShapeDtypeStruct(density.shape, bf16),
            jax.ShapeDtypeStruct((2,), f32),
        ),
        in_specs=[
            pl.BlockSpec(memory_space=pltpu.SMEM),
            pl.BlockSpec(memory_space=pltpu.VMEM),
        ],
        out_specs=(
            pl.BlockSpec(memory_space=pltpu.VMEM),
            pl.BlockSpec(memory_space=pltpu.SMEM),
        ),
        scratch_shapes=[
            pltpu.VMEM((SUPER, TILE), bf16),
            pltpu.VMEM((TILE, SUPER), bf16),
            pltpu.VMEM((SUPER, NSUP * TILE), bf16),
            pltpu.VMEM((NSUP * TILE, SUPER), bf16),
            pltpu.VMEM((SUPER, SUPER), f32),
            pltpu.VMEM((SUPER, 2 * TILE), f32),
            pltpu.VMEM((SUPER, TILE), f32),
            pltpu.VMEM((SUPER, TILE), f32),
            pltpu.VMEM((2, NSUP, 16, BLK), f32),
            pltpu.VMEM((4, 16, BLK), f32),
            dma((2, 2, CHUNKS, 4)), dma((2, 2, CHUNKS, 4)),
            dma((2, 2, 4, CHUNKS)), dma((2, 2, 4, CHUNKS)),
            dma((2, 2, 4)), dma((2, 2, 4)), dma((4,)), dma((4,)),
            dma((4,)), dma((4,)), dma((4,)), dma((4,)),
            dma((3,)), dma((3,)), dma((2,)), dma((2,)),
        ],
        compiler_params=pltpu.CompilerParams(
            collective_id=0, has_side_effects=True, vmem_limit_bytes=40 * 1024 * 1024
        ),
        cost_estimate=pl.CostEstimate(
            flops=2 * SUPER * SUPER * NSUP * TILE, bytes_accessed=2 * 1024 * 1024, transcendentals=0
        ),
    )(pattern, density)


def solution(mesh):
    return jax.shard_map(
        per_device, mesh=mesh, in_specs=(P("row", "col"), P()),
        out_specs=(P("row", "col"), P()), check_vma=False,
    )
```

```python
import jax
import jax.numpy as jnp
from jax import lax
from jax.experimental import pallas as pl
from jax.experimental.pallas import tpu as pltpu
from jax.sharding import PartitionSpec as P

BLK = 128
MESH = pl.DeviceIdType.MESH
TILE = 256
SUPER = 1024
NSUP = 8
CHUNKS = 4
REACH = 3


def ring_order(r, p):
    x, hi = lax.div(r, 2), lax.rem(r, 2)
    xx = lax.rem(x + 2 * p, 4)
    return xx * (1 - hi) + (7 - xx) * hi


def ring_row(h, p):
    hi = lax.div(h, 4)
    xx = h * (1 - hi) + (7 - h) * hi
    return 2 * lax.rem(xx + 2 * p, 4) + hi


def plain_order(p):
    rows = []
    for h in range(8):
        hi = h // 4
        xx = 7 - h if hi else h
        rows.append(2 * ((xx + 2 * p) % 4) + hi)
    return rows


def chains(ring, p, center, parity):
    order = plain_order(p) if ring else list(range(8))
    start = order.index(center)

    def needs(i):
        other = order[(start + i) % 8]
        return other < center if ring else other > center

    offsets = [i for i in range(1, 8) if needs(i)]
    n = len(offsets)
    split = n // 2 if n >= 4 else (0 if parity else n)
    table, firsts = {}, []
    for sign, goals in ((1, offsets[:split]), (-1, [8 - i for i in reversed(offsets[split:])])):
        nodes, now = [], 0
        for goal in goals:
            while goal - now > REACH:
                now += REACH
                nodes.append(now)
            nodes.append(goal)
            now = goal
        places = [order[(start + sign * i) % 8] for i in nodes]
        for depth, place in enumerate(places):
            assert place not in table
            following = places[depth + 1] if depth + 1 < len(places) else place
            table[place] = (depth + 1, following)
        firsts.append(places[0] if places else center)
    table[center] = (0, firsts[0])
    return table, firsts[1]


def packed(ring, p, parity):
    depths, nexts, seconds = [], [], []
    for center in range(8):
        table, second = chains(ring, p, center, parity)
        depths.append(sum(table.get(i, (0, i))[0] * 8**i for i in range(8)))
        nexts.append(sum(table.get(i, (0, i))[1] * 8**i for i in range(8)))
        seconds.append(second)
    return depths, nexts, seconds


DEEPEST = max(
    depth
    for ring in range(2)
    for p in range(2)
    for center in range(8)
    for parity in range(2)
    for depth, _next in chains(ring, p, center, parity)[0].values()
)


def pick(values, index):
    result = jnp.int32(values[0])
    for i, value in enumerate(values):
        result = jnp.where(index == i, jnp.int32(value), result)
    return result


def kernel(
    pat, dens, out, traces,
    tbuf, ttbuf, rowb, colb, part, sibb, ysend, yrecv, tr, trq,
    ring_s, ring_r, inj_s, inj_l, inj_r, tr_s, tr_r, trq_s, trq_r,
    intra_s, intra_r, mirr_s, mirr_r, sib_s, sib_r, y_s, y_r,
):
    r = lax.axis_index("row")
    c = lax.axis_index("col")
    z, s = lax.div(c, 4), lax.rem(c, 4)
    p, q = lax.div(s, 2), lax.rem(s, 2)
    active, diag = r <= z, r == z

    def dev(r_, z_, s_):
        return (r_, 4 * z_ + s_)

    def copy(src, dst, ssem, rsem, device):
        return pltpu.make_async_remote_copy(
            src_ref=src, dst_ref=dst, send_sem=ssem, recv_sem=rsem,
            device_id=device, device_id_type=MESH,
        )

    def wrap(i):
        return lax.rem(i + 8, 8)

    h = ring_order(r, p)
    neighbours = (
        (dev(r, wrap(z + 1), s), dev(r, wrap(z - 1), s)),
        (dev(ring_row(wrap(h + 1), p), z, s), dev(ring_row(wrap(h - 1), p), z, s)),
    )
    others = [lax.rem(s + d, 4) for d in (1, 2, 3)]

    barrier = pltpu.get_barrier_semaphore()
    for i in range(1, 8):
        for device in (dev(r, wrap(z + i), s), dev(wrap(r + i), z, s)):
            pl.semaphore_signal(barrier, inc=1, device_id=device, device_id_type=MESH)
    for o in others:
        pl.semaphore_signal(barrier, inc=1, device_id=dev(r, z, o), device_id_type=MESH)

    def keep(i, j):
        bi, bj = r * 8 + i, c * 2 + j
        return ((pat[bi, bj] != 0) | (bi == bj)) & (bj >= bi), bi == bj

    def quarter(i):
        return pl.ds(pl.multiple_of(i * TILE, TILE), TILE)

    eye = lax.broadcasted_iota(jnp.int32, (BLK, BLK), 0) == lax.broadcasted_iota(jnp.int32, (BLK, BLK), 1)
    first = jnp.zeros((BLK, BLK), jnp.float32)
    second = jnp.zeros((BLK, BLK), jnp.float32)
    for i in range(8):
        for j in range(2):
            kept, same = keep(i, j)
            block = dens[pl.ds(i * BLK, BLK), pl.ds(j * BLK, BLK)].astype(jnp.float32)
            block = jnp.where(kept, block, jnp.zeros_like(block))
            tbuf[pl.ds(i * BLK, BLK), pl.ds(j * BLK, BLK)] = block.astype(jnp.bfloat16)
            first = first + jnp.where(eye & same, block, jnp.zeros_like(block))
            square = block * block
            second = second + jnp.where(same, square, square + square)

            @pl.when(diag)
            def _():
                strict = jnp.where(same, jnp.zeros_like(block), block)
                ttbuf[pl.ds(j * BLK, BLK), pl.ds(i * BLK, BLK)] = strict.T.astype(jnp.bfloat16)

    tr[0, z, 0:8, :] = first.reshape(BLK // 8, 8, BLK).sum(axis=0)
    tr[0, z, 8:16, :] = second.reshape(BLK // 8, 8, BLK).sum(axis=0)

    pl.semaphore_wait(barrier, 17)

    def intra(o):
        return copy(
            tbuf.at[quarter(o), :], colb.at[quarter(r), quarter(s)],
            intra_s.at[o], intra_r.at[s], dev(r, z, o),
        )

    def intra_in(o):
        return copy(
            tbuf.at[quarter(o), :], colb.at[quarter(r), quarter(o)],
            intra_s.at[o], intra_r.at[o], dev(r, z, o),
        )

    def mirror(o):
        return copy(
            ttbuf.at[:, quarter(o)], rowb.at[quarter(s), quarter(z)],
            mirr_s.at[o], mirr_r.at[s], dev(r, z, o),
        )

    def mirror_in(o):
        return copy(
            ttbuf.at[:, quarter(o)], rowb.at[quarter(o), quarter(z)],
            mirr_s.at[o], mirr_r.at[o], dev(r, z, o),
        )

    away, home = (1 - p) * 2, p * 2
    pos = (z, h)

    def chunk(ch):
        return quarter((away if ch < 2 else home) + ch % 2)

    def piece(ring, ch, k):
        return rowb.at[chunk(ch), quarter(k)] if ring == 0 else colb.at[quarter(k), chunk(ch)]

    def at(ring, where):
        return wrap(where) if ring == 0 else ring_row(wrap(where), p)

    def item_at(ring, d, dist):
        return at(ring, pos[ring] - dist if d == 0 else pos[ring] + dist)

    def stored(ring, k):
        return k >= r if ring == 0 else k <= z

    def has_hop(d, ch, t):
        return t <= 3 or (t == 4 and ch % 2 == d)

    def hop(ring, d, ch, t, k):
        ref = piece(ring, ch, k)
        return copy(
            ref, ref, ring_s.at[ring, d, ch, t - 1], ring_r.at[ring, d, ch, t - 1],
            neighbours[ring][d],
        )

    ringdirs = [(a, d) for a in range(2) for d in range(2)]

    def tr_hop(ring, d, t, k):
        ref = tr.at[ring, k]
        return copy(ref, ref, tr_s.at[ring, d, t - 1], tr_r.at[ring, d, t - 1], neighbours[ring][d])

    ahead = [
        [
            [r <= wrap(z + i) if d == 0 else r <= wrap(z - i) for i in range(5)],
            [at(1, h + i) <= z if d == 0 else at(1, h - i) <= z for i in range(5)],
        ]
        for d in range(2)
    ]

    def served(ring, d, i, j):
        result = ahead[d][ring][i]
        for k in range(i + 1, j + 1):
            result = result | ahead[d][ring][k]
        return result

    def goes(ring, d, ch, t):
        return served(ring, d, 1, (4 if ch % 2 == d else 3) - t + 1)

    def comes(ring, d, ch, t):
        return served(ring, d, 0, (4 if ch % 2 == d else 3) - t)

    def own(ring, chs):
        for ch in chs:
            for d in range(2):

                @pl.when(active & goes(ring, d, ch, 1))
                def _():
                    hop(ring, d, ch, 1, item_at(ring, d, 0)).start()

    def tr_own(ring):
        for d in range(2):
            tr_hop(ring, d, 1, item_at(ring, d, 0)).start()

    def natural(chs, t):
        for ch in chs:
            for ring, d in ringdirs:
                if not has_hop(d, ch, t):
                    continue
                k = item_at(ring, d, t)

                @pl.when(stored(ring, k) & comes(ring, d, ch, t))
                def _():
                    hop(ring, d, ch, t, k).wait_recv()

                if has_hop(d, ch, t + 1):

                    @pl.when(stored(ring, k) & goes(ring, d, ch, t + 1))
                    def _():
                        hop(ring, d, ch, t + 1, k).start()

    def tr_step(ring, t):
        for d in range(2):
            if has_hop(d, 0, t):
                k = item_at(ring, d, t)
                tr_hop(ring, d, t, k).wait_recv()
                if has_hop(d, 0, t + 1):
                    tr_hop(ring, d, t + 1, k).start()

    def mirrored(ring, e, d):
        source = (ring_order(r, p), z)[ring]
        k = at(1 - ring, source - d if e == 0 else source + d)
        return k, (k < r if ring == 0 else k > z)

    me = (z, r)
    centers = (r, z)
    route = []
    for ring in range(2):
        for parity in range(2):
            found = [packed(ring, i, parity) for i in range(1 + ring)]
            fields = []
            for field in range(3):
                value = pick(found[0][field], centers[ring])
                if ring:
                    value = jnp.where(p == 0, value, pick(found[1][field], centers[ring]))
                fields.append(value)
            power = pick([8**i for i in range(8)], me[ring])
            fields[:2] = [lax.rem(lax.div(value, power), 8) for value in fields[:2]]
            route.append(fields)

    def inj_hop(ring, e, d, ch, k, to, sem):
        ref = piece(ring, ch, k)
        return copy(
            ref, ref, sem.at[ring, e, d - 1, ch], inj_r.at[ring, e, d - 1, ch],
            dev(r, to, s) if ring == 0 else dev(to, z, s),
        )

    def inject(chs, t):
        for ch in chs:
            for ring in range(2):
                depth, to, second = route[2 * ring + ch % 2]
                d = t - depth
                for e in range(2):
                    k, exists = mirrored(ring, e, d)
                    here = exists & (d >= 1) & (d <= (3 if e else 4))

                    @pl.when(here & (depth > 0))
                    def _():
                        inj_hop(ring, e, d, ch, k, to, inj_s).wait_recv()

                    if t <= 4:

                        @pl.when(here & diag)
                        def _():
                            if ring == 0:
                                rowb[chunk(ch), quarter(k)] = colb[quarter(k), chunk(ch)].T
                            else:
                                colb[quarter(k), chunk(ch)] = rowb[chunk(ch), quarter(k)].T

                    @pl.when(here & (to != me[ring]) & (diag | (depth > 0)))
                    def _():
                        inj_hop(ring, e, d, ch, k, to, inj_s).start()

                    if t <= 4:

                        @pl.when(here & diag & (second != me[ring]))
                        def _():
                            inj_hop(ring, e, d, ch, k, second, inj_l).start()

    def step(chs, t):
        if t <= 4:
            natural(chs, t)
        inject(chs, t)

    def matmul(m0, nq):
        cols = quarter(nq)

        def body(i, carry):
            rows = pl.ds(pl.multiple_of(m0 + i * TILE, TILE), TILE)
            part[rows, cols] = jnp.dot(
                rowb[rows, :], colb[:, cols], preferred_element_type=jnp.float32
            )
            return carry

        lax.fori_loop(0, 2, body, 0)

    sibling = dev(r, z, 2 * p + (1 - q))
    partner = dev(r, z, 2 * (1 - p) + q)
    half = SUPER // 2
    starts = (away * TILE, home * TILE)

    def rows_of(i):
        return pl.ds(pl.multiple_of(starts[i], half), half)

    def sib_away(i):
        rows = rows_of(i)
        return copy(
            part.at[rows, quarter(away + 1 - q)], sibb.at[rows, pl.ds(0, TILE)],
            sib_s.at[i], sib_r.at[i], sibling,
        )

    def sib_home():
        return copy(
            part.at[:, quarter(home + 1 - q)], sibb.at[:, pl.ds(TILE, TILE)],
            sib_s.at[2], sib_r.at[2], sibling,
        )

    def y_copy(i):
        rows = rows_of(i)
        return copy(ysend.at[rows, :], yrecv.at[rows, :], y_s.at[i], y_r.at[i], partner)

    def y_in(i):
        rows = rows_of(1 - i)
        return copy(ysend.at[rows, :], yrecv.at[rows, :], y_s.at[i], y_r.at[i], partner)

    def away_1(i):
        @pl.when(active)
        def _():
            matmul(starts[i], away + 1 - q)
            sib_away(i).start()

    def away_2(i):
        @pl.when(active)
        def _():
            matmul(starts[i], away + q)

    def away_3(i):
        @pl.when(active)
        def _():
            sib_away(i).wait_recv()
            rows = rows_of(i)
            ysend[rows, :] = part[rows, quarter(away + q)] + sibb[rows, pl.ds(0, TILE)]
            y_copy(i).start()

    def trq_copy(o):
        return copy(trq.at[s], trq.at[s], trq_s.at[o], trq_r.at[s], dev(r, z, o))

    def trq_in(o):
        return copy(trq.at[o], trq.at[o], trq_s.at[o], trq_r.at[o], dev(r, z, o))

    def total(ref, n):
        value = ref[0]
        for i in range(1, n):
            value = value + ref[i]
        return value

    @pl.when(active)
    def _():
        for o in others:
            intra(o).start()

    @pl.when(r < z)
    def _():
        rowb[:, quarter(z)] = tbuf[...]
        own(0, (0, 1))
        colb[quarter(r), quarter(s)] = tbuf[quarter(s), :]
        for o in others:
            intra_in(o).wait_recv()

    @pl.when(diag)
    def _():
        for o in others:
            mirror(o).start()
        rowb[quarter(s), quarter(z)] = ttbuf[:, quarter(s)]
        colb[quarter(r), quarter(s)] = tbuf[quarter(s), :]
        for o in others:
            mirror_in(o).wait_recv()
            intra_in(o).wait_recv()
        rowb[:, quarter(z)] = rowb[:, quarter(z)] + tbuf[...]
        own(0, (0, 1))
        colb[quarter(r), :] = colb[quarter(r), :] + ttbuf[...]

    own(1, (0, 1))
    tr_own(0)
    end = 4 + DEEPEST
    for u in range(1, end + 5):
        if u == 3:
            for ring in range(2):
                own(ring, (2, 3))
        if u <= end:
            step((0, 1), u)
        if u <= 4:
            tr_step(0, u)
        if u >= 5:
            step((2, 3), u - 4)
        if u == 5:
            tr[1, r] = total(tr.at[0], 8)
            tr_own(1)
        if 6 <= u <= 9:
            tr_step(1, u - 5)
        if u == 10:
            trq[s] = total(tr.at[1], 8)
            for o in others:
                trq_copy(o).start()
        if u == end + 1:
            away_1(0)
        if u == end + 2:
            away_2(0)
        if u == end + 3:
            away_3(0)
    away_1(1)
    away_2(1)
    away_3(1)

    @pl.when(active)
    def _():
        for i in range(2):
            matmul(i * half, home + 1 - q)
        sib_home().start()
        for i in range(2):
            matmul(i * half, home + q)

    for o in others:
        trq_in(o).wait_recv()
    sums = total(trq, 4)
    traces[0] = jnp.sum(sums[0:8, :]) / (NSUP * SUPER)
    traces[1] = jnp.sum(sums[8:16, :]) / (NSUP * SUPER)

    @pl.when(active)
    def _():
        sib_home().wait_recv()
        for i in range(2):
            y_in(i).wait_recv()
        for i in range(8):
            rows = pl.ds(i * BLK, BLK)
            value = part[rows, quarter(home + q)] + sibb[rows, pl.ds(TILE, TILE)] + yrecv[rows, :]
            for j in range(2):
                kept, _same = keep(i, j)
                block = value[:, j * BLK:(j + 1) * BLK]
                block = jnp.where(kept, block, jnp.zeros_like(block))
                out[rows, pl.ds(j * BLK, BLK)] = block.astype(jnp.bfloat16)

    @pl.when(r > z)
    def _():
        out[...] = jnp.zeros_like(out)

    for ring, d in ringdirs:
        for t in (1, 2, 3, 4):
            k = item_at(ring, d, t - 1)
            if has_hop(d, 0, t):
                tr_hop(ring, d, t, k).wait_send()

            for ch in range(CHUNKS):
                if has_hop(d, ch, t):

                    @pl.when(stored(ring, k) & goes(ring, d, ch, t))
                    def _():
                        hop(ring, d, ch, t, k).wait_send()

    for ch in range(CHUNKS):
        for ring in range(2):
            depth, to, second = route[2 * ring + ch % 2]
            for e in range(2):
                for d in range(1, 4 if e else 5):
                    k, exists = mirrored(ring, e, d)

                    @pl.when(exists & (to != me[ring]) & (diag | (depth > 0)))
                    def _():
                        inj_hop(ring, e, d, ch, k, to, inj_s).wait_send()

                    @pl.when(exists & diag & (second != me[ring]))
                    def _():
                        inj_hop(ring, e, d, ch, k, second, inj_l).wait_send()

    for o in others:
        trq_copy(o).wait_send()

    @pl.when(active)
    def _():
        for i in range(2):
            sib_away(i).wait_send()
            y_copy(i).wait_send()
        sib_home().wait_send()
        for o in others:
            intra(o).wait_send()

    @pl.when(diag)
    def _():
        for o in others:
            mirror(o).wait_send()


def per_device(density, pattern):
    dma = pltpu.SemaphoreType.DMA
    f32, bf16 = jnp.float32, jnp.bfloat16
    return pl.pallas_call(
        kernel,
        out_shape=(
            jax.ShapeDtypeStruct(density.shape, bf16),
            jax.ShapeDtypeStruct((2,), f32),
        ),
        in_specs=[
            pl.BlockSpec(memory_space=pltpu.SMEM),
            pl.BlockSpec(memory_space=pltpu.VMEM),
        ],
        out_specs=(
            pl.BlockSpec(memory_space=pltpu.VMEM),
            pl.BlockSpec(memory_space=pltpu.SMEM),
        ),
        scratch_shapes=[
            pltpu.VMEM((SUPER, TILE), bf16),
            pltpu.VMEM((TILE, SUPER), bf16),
            pltpu.VMEM((SUPER, NSUP * TILE), bf16),
            pltpu.VMEM((NSUP * TILE, SUPER), bf16),
            pltpu.VMEM((SUPER, SUPER), f32),
            pltpu.VMEM((SUPER, 2 * TILE), f32),
            pltpu.VMEM((SUPER, TILE), f32),
            pltpu.VMEM((SUPER, TILE), f32),
            pltpu.VMEM((2, NSUP, 16, BLK), f32),
            pltpu.VMEM((4, 16, BLK), f32),
            dma((2, 2, CHUNKS, 4)), dma((2, 2, CHUNKS, 4)),
            dma((2, 2, 4, CHUNKS)), dma((2, 2, 4, CHUNKS)), dma((2, 2, 4, CHUNKS)),
            dma((2, 2, 4)), dma((2, 2, 4)), dma((4,)), dma((4,)),
            dma((4,)), dma((4,)), dma((4,)), dma((4,)),
            dma((3,)), dma((3,)), dma((2,)), dma((2,)),
        ],
        compiler_params=pltpu.CompilerParams(
            collective_id=0, has_side_effects=True, vmem_limit_bytes=40 * 1024 * 1024
        ),
        cost_estimate=pl.CostEstimate(
            flops=2 * SUPER * SUPER * NSUP * TILE, bytes_accessed=2 * 1024 * 1024, transcendentals=0
        ),
    )(pattern, density)


def solution(mesh):
    return jax.shard_map(
        per_device, mesh=mesh, in_specs=(P("row", "col"), P()),
        out_specs=(P("row", "col"), P()), check_vma=False,
    )
```

```python
import jax
import jax.numpy as jnp
from jax import lax
from jax.experimental import pallas as pl
from jax.experimental.pallas import tpu as pltpu
from jax.sharding import PartitionSpec as P

BLK = 128
MESH = pl.DeviceIdType.MESH
TILE = 256
SUPER = 1024
NSUP = 8
CHUNKS = 4
LAG = 3


def ring_order(r, p):
    x, hi = lax.div(r, 2), lax.rem(r, 2)
    xx = lax.rem(x + 2 * p, 4)
    return xx * (1 - hi) + (7 - xx) * hi


def ring_row(h, p):
    hi = lax.div(h, 4)
    xx = h * (1 - hi) + (7 - h) * hi
    return 2 * lax.rem(xx + 2 * p, 4) + hi


CHAINS = (
    (
        (
            (((), ()), ((), ())),
            (((7, 6, 5,), (2, 3, 4,)), ((7, 6, 5, 4,), (2, 3,))),
            (((7, 6, 5,), (3, 4,)), ((7, 6, 5,), (3, 4,))),
            (((2, 7, 6,), (4, 5,)), ((0, 7, 6, 5,), (4,))),
            (((), (1, 7, 6, 5,)), ((2, 7,), (5, 6,))),
            (((), (2, 7, 6,)), ((6, 7,), ())),
            (((), (3, 2, 7,)), ((7,), ())),
            (((), ()), ((), ())),
        ),
    ),
    (
        (
            (((), ()), ((), ())),
            (((6, 0,), ()), ((), (2, 0,))),
            (((), (0, 7, 1,)), ((3, 1,), (6, 0,))),
            (((4, 2, 0,), (1,)), ((1,), (4, 2, 0,))),
            (((2, 3, 1,), (0,)), ((2, 0,), (5, 3, 1,))),
            (((3, 1,), (4, 2, 0,)), ((2, 0, 4,), (3, 1,))),
            (((7, 5, 3, 1,), (0, 2, 4,)), ((5, 3, 1,), (4, 2, 0,))),
            (((), ()), ((), ())),
        ),
        (
            (((), ()), ((), ())),
            (((), (4, 0,)), ((0,), ())),
            (((), (0, 1,)), ((5, 1, 0,), ())),
            (((), (1, 0, 2,)), ((2, 0, 1,), ())),
            (((0, 7, 1, 3,), (2,)), ((2, 6, 0,), (5, 3, 7, 1,))),
            (((4, 2, 0,), (3, 1,)), ((3, 2, 4,), (1, 0,))),
            (((4, 2,), (0, 1, 5, 3,)), ((0, 2, 4,), (7, 1, 3, 5,))),
            (((), ()), ((), ())),
        ),
    ),
)


def chains(ring, p, center, parity):
    table, firsts = {}, []
    for places in CHAINS[ring][p][center][parity]:
        for depth, place in enumerate(places):
            assert place not in table
            following = places[depth + 1] if depth + 1 < len(places) else place
            table[place] = (depth + 1, following)
        firsts.append(places[0] if places else center)
    table[center] = (0, firsts[0])
    return table, firsts[1]


def packed(ring, p, parity):
    depths, nexts, seconds = [], [], []
    for center in range(8):
        table, second = chains(ring, p, center, parity)
        depths.append(sum(table.get(i, (0, i))[0] * 8**i for i in range(8)))
        nexts.append(sum(table.get(i, (0, i))[1] * 8**i for i in range(8)))
        seconds.append(second)
    return depths, nexts, seconds


DEEPEST = max(
    depth
    for ring in range(2)
    for p in range(1 + ring)
    for center in range(8)
    for parity in range(2)
    for depth, _next in chains(ring, p, center, parity)[0].values()
)


def pick(values, index):
    result = jnp.int32(values[0])
    for i, value in enumerate(values):
        result = jnp.where(index == i, jnp.int32(value), result)
    return result


def kernel(
    pat, dens, out, traces,
    tbuf, ttbuf, rowb, colb, part, sibb, ysend, yrecv, tr, trq,
    ring_s, ring_r, inj_s, inj_l, inj_r, tr_s, tr_r, trq_s, trq_r,
    intra_s, intra_r, mirr_s, mirr_r, sib_s, sib_r, y_s, y_r,
):
    r = lax.axis_index("row")
    c = lax.axis_index("col")
    z, s = lax.div(c, 4), lax.rem(c, 4)
    p, q = lax.div(s, 2), lax.rem(s, 2)
    active, diag = r <= z, r == z

    def dev(r_, z_, s_):
        return (r_, 4 * z_ + s_)

    def copy(src, dst, ssem, rsem, device):
        return pltpu.make_async_remote_copy(
            src_ref=src, dst_ref=dst, send_sem=ssem, recv_sem=rsem,
            device_id=device, device_id_type=MESH,
        )

    def wrap(i):
        return lax.rem(i + 8, 8)

    h = ring_order(r, p)
    neighbours = (
        (dev(r, wrap(z + 1), s), dev(r, wrap(z - 1), s)),
        (dev(ring_row(wrap(h + 1), p), z, s), dev(ring_row(wrap(h - 1), p), z, s)),
    )
    others = [lax.rem(s + d, 4) for d in (1, 2, 3)]

    barrier = pltpu.get_barrier_semaphore()
    for i in range(1, 8):
        for device in (dev(r, wrap(z + i), s), dev(wrap(r + i), z, s)):
            pl.semaphore_signal(barrier, inc=1, device_id=device, device_id_type=MESH)
    for o in others:
        pl.semaphore_signal(barrier, inc=1, device_id=dev(r, z, o), device_id_type=MESH)

    def keep(i, j):
        bi, bj = r * 8 + i, c * 2 + j
        return ((pat[bi, bj] != 0) | (bi == bj)) & (bj >= bi), bi == bj

    def quarter(i):
        return pl.ds(pl.multiple_of(i * TILE, TILE), TILE)

    eye = lax.broadcasted_iota(jnp.int32, (BLK, BLK), 0) == lax.broadcasted_iota(jnp.int32, (BLK, BLK), 1)
    first = jnp.zeros((BLK, BLK), jnp.float32)
    second = jnp.zeros((BLK, BLK), jnp.float32)
    for i in range(8):
        for j in range(2):
            kept, same = keep(i, j)
            block = dens[pl.ds(i * BLK, BLK), pl.ds(j * BLK, BLK)].astype(jnp.float32)
            block = jnp.where(kept, block, jnp.zeros_like(block))
            tbuf[pl.ds(i * BLK, BLK), pl.ds(j * BLK, BLK)] = block.astype(jnp.bfloat16)
            first = first + jnp.where(eye & same, block, jnp.zeros_like(block))
            square = block * block
            second = second + jnp.where(same, square, square + square)

            @pl.when(diag)
            def _():
                strict = jnp.where(same, jnp.zeros_like(block), block)
                ttbuf[pl.ds(j * BLK, BLK), pl.ds(i * BLK, BLK)] = strict.T.astype(jnp.bfloat16)

    tr[0, z, 0:8, :] = first.reshape(BLK // 8, 8, BLK).sum(axis=0)
    tr[0, z, 8:16, :] = second.reshape(BLK // 8, 8, BLK).sum(axis=0)

    pl.semaphore_wait(barrier, 17)

    def intra(o):
        return copy(
            tbuf.at[quarter(o), :], colb.at[quarter(r), quarter(s)],
            intra_s.at[o], intra_r.at[s], dev(r, z, o),
        )

    def intra_in(o):
        return copy(
            tbuf.at[quarter(o), :], colb.at[quarter(r), quarter(o)],
            intra_s.at[o], intra_r.at[o], dev(r, z, o),
        )

    def mirror(o):
        return copy(
            ttbuf.at[:, quarter(o)], rowb.at[quarter(s), quarter(z)],
            mirr_s.at[o], mirr_r.at[s], dev(r, z, o),
        )

    def mirror_in(o):
        return copy(
            ttbuf.at[:, quarter(o)], rowb.at[quarter(o), quarter(z)],
            mirr_s.at[o], mirr_r.at[o], dev(r, z, o),
        )

    away, home = (1 - p) * 2, p * 2
    pos = (z, h)

    def chunk(ch):
        return quarter((away if ch < 2 else home) + ch % 2)

    def piece(ring, ch, k):
        return rowb.at[chunk(ch), quarter(k)] if ring == 0 else colb.at[quarter(k), chunk(ch)]

    def at(ring, where):
        return wrap(where) if ring == 0 else ring_row(wrap(where), p)

    def item_at(ring, d, dist):
        return at(ring, pos[ring] - dist if d == 0 else pos[ring] + dist)

    def stored(ring, k):
        return k >= r if ring == 0 else k <= z

    def has_hop(d, ch, t):
        return t <= 3 or (t == 4 and ch % 2 == d)

    def hop(ring, d, ch, t, k):
        ref = piece(ring, ch, k)
        return copy(
            ref, ref, ring_s.at[ring, d, ch, t - 1], ring_r.at[ring, d, ch, t - 1],
            neighbours[ring][d],
        )

    ringdirs = [(a, d) for a in range(2) for d in range(2)]

    def tr_hop(ring, d, t, k):
        ref = tr.at[ring, k]
        return copy(ref, ref, tr_s.at[ring, d, t - 1], tr_r.at[ring, d, t - 1], neighbours[ring][d])

    ahead = [
        [
            [r <= wrap(z + i) if d == 0 else r <= wrap(z - i) for i in range(5)],
            [at(1, h + i) <= z if d == 0 else at(1, h - i) <= z for i in range(5)],
        ]
        for d in range(2)
    ]

    def served(ring, d, i, j):
        result = ahead[d][ring][i]
        for k in range(i + 1, j + 1):
            result = result | ahead[d][ring][k]
        return result

    def goes(ring, d, ch, t):
        return served(ring, d, 1, (4 if ch % 2 == d else 3) - t + 1)

    def comes(ring, d, ch, t):
        return served(ring, d, 0, (4 if ch % 2 == d else 3) - t)

    def own(ring, chs):
        for ch in chs:
            for d in range(2):

                @pl.when(active & goes(ring, d, ch, 1))
                def _():
                    hop(ring, d, ch, 1, item_at(ring, d, 0)).start()

    def tr_own(ring):
        for d in range(2):
            tr_hop(ring, d, 1, item_at(ring, d, 0)).start()

    def natural(chs, t):
        for ch in chs:
            for ring, d in ringdirs:
                if not has_hop(d, ch, t):
                    continue
                k = item_at(ring, d, t)

                @pl.when(stored(ring, k) & comes(ring, d, ch, t))
                def _():
                    hop(ring, d, ch, t, k).wait_recv()

                if has_hop(d, ch, t + 1):

                    @pl.when(stored(ring, k) & goes(ring, d, ch, t + 1))
                    def _():
                        hop(ring, d, ch, t + 1, k).start()

    def tr_step(ring, t):
        for d in range(2):
            if has_hop(d, 0, t):
                k = item_at(ring, d, t)
                tr_hop(ring, d, t, k).wait_recv()
                if has_hop(d, 0, t + 1):
                    tr_hop(ring, d, t + 1, k).start()

    def mirrored(ring, e, d):
        source = (ring_order(r, p), z)[ring]
        k = at(1 - ring, source - d if e == 0 else source + d)
        return k, (k < r if ring == 0 else k > z)

    me = (z, r)
    centers = (r, z)
    route = []
    for ring in range(2):
        for parity in range(2):
            found = [packed(ring, i, parity) for i in range(1 + ring)]
            fields = []
            for field in range(3):
                value = pick(found[0][field], centers[ring])
                if ring:
                    value = jnp.where(p == 0, value, pick(found[1][field], centers[ring]))
                fields.append(value)
            power = pick([8**i for i in range(8)], me[ring])
            fields[:2] = [lax.rem(lax.div(value, power), 8) for value in fields[:2]]
            route.append(fields)

    def inj_hop(ring, e, d, ch, k, to, sem):
        ref = piece(ring, ch, k)
        return copy(
            ref, ref, sem.at[ring, e, d - 1, ch], inj_r.at[ring, e, d - 1, ch],
            dev(r, to, s) if ring == 0 else dev(to, z, s),
        )

    def inject(chs, t):
        for ch in chs:
            for ring in range(2):
                depth, to, second = route[2 * ring + ch % 2]
                d = t - depth
                for e in range(2):
                    k, exists = mirrored(ring, e, d)
                    here = exists & (d >= 1) & (d <= (3 if e else 4))

                    @pl.when(here & (depth > 0))
                    def _():
                        inj_hop(ring, e, d, ch, k, to, inj_s).wait_recv()

                    if t <= 4:

                        @pl.when(here & diag)
                        def _():
                            if ring == 0:
                                rowb[chunk(ch), quarter(k)] = colb[quarter(k), chunk(ch)].T
                            else:
                                colb[quarter(k), chunk(ch)] = rowb[chunk(ch), quarter(k)].T

                    @pl.when(here & (to != me[ring]) & (diag | (depth > 0)))
                    def _():
                        inj_hop(ring, e, d, ch, k, to, inj_s).start()

                    if t <= 4:

                        @pl.when(here & diag & (second != me[ring]))
                        def _():
                            inj_hop(ring, e, d, ch, k, second, inj_l).start()

    def matmul(m0, nq):
        cols = quarter(nq)

        def body(i, carry):
            rows = pl.ds(pl.multiple_of(m0 + i * TILE, TILE), TILE)
            part[rows, cols] = jnp.dot(
                rowb[rows, :], colb[:, cols], preferred_element_type=jnp.float32
            )
            return carry

        lax.fori_loop(0, 2, body, 0)

    sibling = dev(r, z, 2 * p + (1 - q))
    partner = dev(r, z, 2 * (1 - p) + q)
    half = SUPER // 2
    starts = (away * TILE, home * TILE)

    def rows_of(i):
        return pl.ds(pl.multiple_of(starts[i], half), half)

    def sib_away(i):
        rows = rows_of(i)
        return copy(
            part.at[rows, quarter(away + 1 - q)], sibb.at[rows, pl.ds(0, TILE)],
            sib_s.at[i], sib_r.at[i], sibling,
        )

    def sib_home():
        return copy(
            part.at[:, quarter(home + 1 - q)], sibb.at[:, pl.ds(TILE, TILE)],
            sib_s.at[2], sib_r.at[2], sibling,
        )

    def y_copy(i):
        rows = rows_of(i)
        return copy(ysend.at[rows, :], yrecv.at[rows, :], y_s.at[i], y_r.at[i], partner)

    def y_in(i):
        rows = rows_of(1 - i)
        return copy(ysend.at[rows, :], yrecv.at[rows, :], y_s.at[i], y_r.at[i], partner)

    def away_1(i):
        @pl.when(active)
        def _():
            matmul(starts[i], away + 1 - q)
            sib_away(i).start()

    def away_2(i):
        @pl.when(active)
        def _():
            matmul(starts[i], away + q)

    def away_3(i):
        @pl.when(active)
        def _():
            sib_away(i).wait_recv()
            rows = rows_of(i)
            ysend[rows, :] = part[rows, quarter(away + q)] + sibb[rows, pl.ds(0, TILE)]
            y_copy(i).start()

    def trq_copy(o):
        return copy(trq.at[s], trq.at[s], trq_s.at[o], trq_r.at[s], dev(r, z, o))

    def trq_in(o):
        return copy(trq.at[o], trq.at[o], trq_s.at[o], trq_r.at[o], dev(r, z, o))

    def total(ref, n):
        value = ref[0]
        for i in range(1, n):
            value = value + ref[i]
        return value

    @pl.when(active)
    def _():
        for o in others:
            intra(o).start()

    @pl.when(r < z)
    def _():
        rowb[:, quarter(z)] = tbuf[...]
        own(0, (0, 1))
        colb[quarter(r), quarter(s)] = tbuf[quarter(s), :]
        for o in others:
            intra_in(o).wait_recv()

    @pl.when(diag)
    def _():
        for o in others:
            mirror(o).start()
        rowb[quarter(s), quarter(z)] = ttbuf[:, quarter(s)]
        colb[quarter(r), quarter(s)] = tbuf[quarter(s), :]
        for o in others:
            mirror_in(o).wait_recv()
            intra_in(o).wait_recv()
        rowb[:, quarter(z)] = rowb[:, quarter(z)] + tbuf[...]
        own(0, (0, 1))
        colb[quarter(r), :] = colb[quarter(r), :] + ttbuf[...]

    own(1, (0, 1))
    tr_own(0)
    end = 4 + DEEPEST
    for u in range(1, end + LAG + 1):
        if u == LAG - 1:
            for ring in range(2):
                own(ring, (2, 3))
        if u <= 4:
            natural((0, 1), u)
        if 1 <= u - LAG <= 4:
            natural((2, 3), u - LAG)
        if u <= end:
            inject((0, 1), u)
        if u > LAG:
            inject((2, 3), u - LAG)
        if u <= 4:
            tr_step(0, u)
        if u == 5:
            tr[1, r] = total(tr.at[0], 8)
            tr_own(1)
        if 6 <= u <= 9:
            tr_step(1, u - 5)
        if u == 10:
            trq[s] = total(tr.at[1], 8)
            for o in others:
                trq_copy(o).start()
        if u == end + 1:
            away_1(0)
        if u == end + 2:
            away_2(0)
        if u == end + 3:
            away_3(0)
    away_1(1)
    away_2(1)
    away_3(1)

    @pl.when(active)
    def _():
        for i in range(2):
            matmul(i * half, home + 1 - q)
        sib_home().start()
        for i in range(2):
            matmul(i * half, home + q)

    for o in others:
        trq_in(o).wait_recv()
    sums = total(trq, 4)
    traces[0] = jnp.sum(sums[0:8, :]) / (NSUP * SUPER)
    traces[1] = jnp.sum(sums[8:16, :]) / (NSUP * SUPER)

    @pl.when(active)
    def _():
        sib_home().wait_recv()
        for i in range(2):
            y_in(i).wait_recv()
        for i in range(8):
            rows = pl.ds(i * BLK, BLK)
            value = part[rows, quarter(home + q)] + sibb[rows, pl.ds(TILE, TILE)] + yrecv[rows, :]
            for j in range(2):
                kept, _same = keep(i, j)
                block = value[:, j * BLK:(j + 1) * BLK]
                block = jnp.where(kept, block, jnp.zeros_like(block))
                out[rows, pl.ds(j * BLK, BLK)] = block.astype(jnp.bfloat16)

    @pl.when(r > z)
    def _():
        out[...] = jnp.zeros_like(out)

    for ring, d in ringdirs:
        for t in (1, 2, 3, 4):
            k = item_at(ring, d, t - 1)
            if has_hop(d, 0, t):
                tr_hop(ring, d, t, k).wait_send()

            for ch in range(CHUNKS):
                if has_hop(d, ch, t):

                    @pl.when(stored(ring, k) & goes(ring, d, ch, t))
                    def _():
                        hop(ring, d, ch, t, k).wait_send()

    for ch in range(CHUNKS):
        for ring in range(2):
            depth, to, second = route[2 * ring + ch % 2]
            for e in range(2):
                for d in range(1, 4 if e else 5):
                    k, exists = mirrored(ring, e, d)

                    @pl.when(exists & (to != me[ring]) & (diag | (depth > 0)))
                    def _():
                        inj_hop(ring, e, d, ch, k, to, inj_s).wait_send()

                    @pl.when(exists & diag & (second != me[ring]))
                    def _():
                        inj_hop(ring, e, d, ch, k, second, inj_l).wait_send()

    for o in others:
        trq_copy(o).wait_send()

    @pl.when(active)
    def _():
        for i in range(2):
            sib_away(i).wait_send()
            y_copy(i).wait_send()
        sib_home().wait_send()
        for o in others:
            intra(o).wait_send()

    @pl.when(diag)
    def _():
        for o in others:
            mirror(o).wait_send()


def per_device(density, pattern):
    dma = pltpu.SemaphoreType.DMA
    f32, bf16 = jnp.float32, jnp.bfloat16
    return pl.pallas_call(
        kernel,
        out_shape=(
            jax.ShapeDtypeStruct(density.shape, bf16),
            jax.ShapeDtypeStruct((2,), f32),
        ),
        in_specs=[
            pl.BlockSpec(memory_space=pltpu.SMEM),
            pl.BlockSpec(memory_space=pltpu.VMEM),
        ],
        out_specs=(
            pl.BlockSpec(memory_space=pltpu.VMEM),
            pl.BlockSpec(memory_space=pltpu.SMEM),
        ),
        scratch_shapes=[
            pltpu.VMEM((SUPER, TILE), bf16),
            pltpu.VMEM((TILE, SUPER), bf16),
            pltpu.VMEM((SUPER, NSUP * TILE), bf16),
            pltpu.VMEM((NSUP * TILE, SUPER), bf16),
            pltpu.VMEM((SUPER, SUPER), f32),
            pltpu.VMEM((SUPER, 2 * TILE), f32),
            pltpu.VMEM((SUPER, TILE), f32),
            pltpu.VMEM((SUPER, TILE), f32),
            pltpu.VMEM((2, NSUP, 16, BLK), f32),
            pltpu.VMEM((4, 16, BLK), f32),
            dma((2, 2, CHUNKS, 4)), dma((2, 2, CHUNKS, 4)),
            dma((2, 2, 4, CHUNKS)), dma((2, 2, 4, CHUNKS)), dma((2, 2, 4, CHUNKS)),
            dma((2, 2, 4)), dma((2, 2, 4)), dma((4,)), dma((4,)),
            dma((4,)), dma((4,)), dma((4,)), dma((4,)),
            dma((3,)), dma((3,)), dma((2,)), dma((2,)),
        ],
        compiler_params=pltpu.CompilerParams(
            collective_id=0, has_side_effects=True, vmem_limit_bytes=40 * 1024 * 1024
        ),
        cost_estimate=pl.CostEstimate(
            flops=2 * SUPER * SUPER * NSUP * TILE, bytes_accessed=2 * 1024 * 1024, transcendentals=0
        ),
    )(pattern, density)


def solution(mesh):
    return jax.shard_map(
        per_device, mesh=mesh, in_specs=(P("row", "col"), P()),
        out_specs=(P("row", "col"), P()), check_vma=False,
    )
```

```python
import jax
import jax.numpy as jnp
from jax import lax
from jax.experimental import pallas as pl
from jax.experimental.pallas import tpu as pltpu
from jax.sharding import PartitionSpec as P

BLK = 128
MESH = pl.DeviceIdType.MESH
TILE = 256
SUPER = 1024
NSUP = 8
CHUNKS = 4
LAG = 2


def ring_order(r, p):
    x, hi = lax.div(r, 2), lax.rem(r, 2)
    xx = lax.rem(x + 2 * p, 4)
    return xx * (1 - hi) + (7 - xx) * hi


def ring_row(h, p):
    hi = lax.div(h, 4)
    xx = h * (1 - hi) + (7 - h) * hi
    return 2 * lax.rem(xx + 2 * p, 4) + hi


CHAINS = (
    (
        (
            (((), ()), ((), ())),
            (((7, 6, 5,), (2, 3, 4,)), ((7, 6, 5, 4,), (2, 3,))),
            (((7, 6, 5,), (3, 4,)), ((7, 6, 5,), (3, 4,))),
            (((2, 7, 6,), (4, 5,)), ((0, 7, 6, 5,), (4,))),
            (((), (1, 7, 6, 5,)), ((2, 7,), (5, 6,))),
            (((), (2, 7, 6,)), ((6, 7,), ())),
            (((), (3, 2, 7,)), ((7,), ())),
            (((), ()), ((), ())),
        ),
    ),
    (
        (
            (((), ()), ((), ())),
            (((6, 0,), ()), ((), (2, 0,))),
            (((), (0, 7, 1,)), ((3, 1,), (6, 0,))),
            (((4, 2, 0,), (1,)), ((1,), (4, 2, 0,))),
            (((2, 3, 1,), (0,)), ((2, 0,), (5, 3, 1,))),
            (((3, 1,), (4, 2, 0,)), ((2, 0, 4,), (3, 1,))),
            (((7, 5, 3, 1,), (0, 2, 4,)), ((5, 3, 1,), (4, 2, 0,))),
            (((), ()), ((), ())),
        ),
        (
            (((), ()), ((), ())),
            (((), (4, 0,)), ((0,), ())),
            (((), (0, 1,)), ((5, 1, 0,), ())),
            (((), (1, 0, 2,)), ((2, 0, 1,), ())),
            (((0, 7, 1, 3,), (2,)), ((2, 6, 0,), (5, 3, 7, 1,))),
            (((4, 2, 0,), (3, 1,)), ((3, 2, 4,), (1, 0,))),
            (((4, 2,), (0, 1, 5, 3,)), ((0, 2, 4,), (7, 1, 3, 5,))),
            (((), ()), ((), ())),
        ),
    ),
)


def chains(ring, p, center, parity):
    table, firsts = {}, []
    for places in CHAINS[ring][p][center][parity]:
        for depth, place in enumerate(places):
            assert place not in table
            following = places[depth + 1] if depth + 1 < len(places) else place
            table[place] = (depth + 1, following)
        firsts.append(places[0] if places else center)
    table[center] = (0, firsts[0])
    return table, firsts[1]


def packed(ring, p, parity):
    depths, nexts, seconds = [], [], []
    for center in range(8):
        table, second = chains(ring, p, center, parity)
        depths.append(sum(table.get(i, (0, i))[0] * 8**i for i in range(8)))
        nexts.append(sum(table.get(i, (0, i))[1] * 8**i for i in range(8)))
        seconds.append(second)
    return depths, nexts, seconds


DEEPEST = max(
    depth
    for ring in range(2)
    for p in range(1 + ring)
    for center in range(8)
    for parity in range(2)
    for depth, _next in chains(ring, p, center, parity)[0].values()
)


def pick(values, index):
    result = jnp.int32(values[0])
    for i, value in enumerate(values):
        result = jnp.where(index == i, jnp.int32(value), result)
    return result


def kernel(
    pat_in, dens_in, out, traces,
    pat, dens, in_sem,
    tbuf, rowb, colb, part, sibb, ysend, yrecv, tr, trq,
    ring_s, ring_r, inj_s, inj_l, inj_r, tr_s, tr_r, trq_s, trq_r,
    intra_s, intra_r, sib_s, sib_r, y_s, y_r,
):
    r = lax.axis_index("row")
    c = lax.axis_index("col")
    z, s = lax.div(c, 4), lax.rem(c, 4)
    p, q = lax.div(s, 2), lax.rem(s, 2)
    active, diag = r <= z, r == z

    def dev(r_, z_, s_):
        return (r_, 4 * z_ + s_)

    def copy(src, dst, ssem, rsem, device):
        return pltpu.make_async_remote_copy(
            src_ref=src, dst_ref=dst, send_sem=ssem, recv_sem=rsem,
            device_id=device, device_id_type=MESH,
        )

    def wrap(i):
        return lax.rem(i + 8, 8)

    h = ring_order(r, p)
    neighbours = (
        (dev(r, wrap(z + 1), s), dev(r, wrap(z - 1), s)),
        (dev(ring_row(wrap(h + 1), p), z, s), dev(ring_row(wrap(h - 1), p), z, s)),
    )
    others = [lax.rem(s + d, 4) for d in (1, 2, 3)]

    barrier = pltpu.get_barrier_semaphore()
    for i in range(1, 8):
        for device in (dev(r, wrap(z + i), s), dev(wrap(r + i), z, s)):
            pl.semaphore_signal(barrier, inc=1, device_id=device, device_id_type=MESH)
    for o in others:
        pl.semaphore_signal(barrier, inc=1, device_id=dev(r, z, o), device_id_type=MESH)

    inputs = (
        pltpu.make_async_copy(pat_in, pat, in_sem.at[0]),
        pltpu.make_async_copy(dens_in, dens, in_sem.at[1]),
    )
    for item in inputs:
        item.start()
    for item in inputs:
        item.wait()

    def keep(i, j):
        bi, bj = r * 8 + i, c * 2 + j
        return ((pat[bi, bj] != 0) | (bi == bj)) & (bj >= bi), bi == bj

    def quarter(i):
        return pl.ds(pl.multiple_of(i * TILE, TILE), TILE)

    eye = lax.broadcasted_iota(jnp.int32, (BLK, BLK), 0) == lax.broadcasted_iota(jnp.int32, (BLK, BLK), 1)
    first = jnp.zeros((BLK, BLK), jnp.float32)
    second = jnp.zeros((BLK, BLK), jnp.float32)
    for i in range(8):
        for j in range(2):
            kept, same = keep(i, j)
            block = dens[pl.ds(i * BLK, BLK), pl.ds(j * BLK, BLK)].astype(jnp.float32)
            block = jnp.where(kept, block, jnp.zeros_like(block))
            tbuf[pl.ds(i * BLK, BLK), pl.ds(j * BLK, BLK)] = block.astype(jnp.bfloat16)
            first = first + jnp.where(eye & same, block, jnp.zeros_like(block))
            square = block * block
            second = second + jnp.where(same, square, square + square)

    tr[0, z, 0:8, :] = first.reshape(BLK // 8, 8, BLK).sum(axis=0)
    tr[0, z, 8:16, :] = second.reshape(BLK // 8, 8, BLK).sum(axis=0)

    pl.semaphore_wait(barrier, 17)

    def intra(o):
        return copy(
            tbuf.at[quarter(o), :], colb.at[quarter(r), quarter(s)],
            intra_s.at[o], intra_r.at[s], dev(r, z, o),
        )

    def intra_in(o):
        return copy(
            tbuf.at[quarter(o), :], colb.at[quarter(r), quarter(o)],
            intra_s.at[o], intra_r.at[o], dev(r, z, o),
        )

    away, home = (1 - p) * 2, p * 2
    pos = (z, h)

    def chunk(ch):
        return quarter((away if ch < 2 else home) + ch % 2)

    def piece(ring, ch, k):
        return rowb.at[chunk(ch), quarter(k)] if ring == 0 else colb.at[quarter(k), chunk(ch)]

    def at(ring, where):
        return wrap(where) if ring == 0 else ring_row(wrap(where), p)

    def item_at(ring, d, dist):
        return at(ring, pos[ring] - dist if d == 0 else pos[ring] + dist)

    def stored(ring, k):
        return k >= r if ring == 0 else k <= z

    def has_hop(d, ch, t):
        return t <= 3 or (t == 4 and ch % 2 == d)

    def hop(ring, d, ch, t, k):
        ref = piece(ring, ch, k)
        return copy(
            ref, ref, ring_s.at[ring, d, ch, t - 1], ring_r.at[ring, d, ch, t - 1],
            neighbours[ring][d],
        )

    ringdirs = [(a, d) for a in range(2) for d in range(2)]

    def tr_hop(ring, d, t, k):
        ref = tr.at[ring, k]
        return copy(ref, ref, tr_s.at[ring, d, t - 1], tr_r.at[ring, d, t - 1], neighbours[ring][d])

    ahead = [
        [
            [r <= wrap(z + i) if d == 0 else r <= wrap(z - i) for i in range(5)],
            [at(1, h + i) <= z if d == 0 else at(1, h - i) <= z for i in range(5)],
        ]
        for d in range(2)
    ]

    def served(ring, d, i, j):
        result = ahead[d][ring][i]
        for k in range(i + 1, j + 1):
            result = result | ahead[d][ring][k]
        return result

    def goes(ring, d, ch, t):
        return served(ring, d, 1, (4 if ch % 2 == d else 3) - t + 1)

    def comes(ring, d, ch, t):
        return served(ring, d, 0, (4 if ch % 2 == d else 3) - t)

    def own(ring, chs):
        for ch in chs:
            for d in range(2):

                @pl.when(active & goes(ring, d, ch, 1))
                def _():
                    hop(ring, d, ch, 1, item_at(ring, d, 0)).start()

    def tr_own(ring):
        for d in range(2):
            tr_hop(ring, d, 1, item_at(ring, d, 0)).start()

    def natural(chs, t):
        for ch in chs:
            for ring, d in ringdirs:
                if not has_hop(d, ch, t):
                    continue
                k = item_at(ring, d, t)

                @pl.when(stored(ring, k) & comes(ring, d, ch, t))
                def _():
                    hop(ring, d, ch, t, k).wait_recv()

                if has_hop(d, ch, t + 1):

                    @pl.when(stored(ring, k) & goes(ring, d, ch, t + 1))
                    def _():
                        hop(ring, d, ch, t + 1, k).start()

    def tr_step(ring, t):
        for d in range(2):
            if has_hop(d, 0, t):
                k = item_at(ring, d, t)
                tr_hop(ring, d, t, k).wait_recv()
                if has_hop(d, 0, t + 1):
                    tr_hop(ring, d, t + 1, k).start()

    def mirrored(ring, e, d):
        source = (ring_order(r, p), z)[ring]
        k = at(1 - ring, source - d if e == 0 else source + d)
        return k, (k < r if ring == 0 else k > z)

    me = (z, r)
    centers = (r, z)
    route = []
    for ring in range(2):
        for parity in range(2):
            found = [packed(ring, i, parity) for i in range(1 + ring)]
            fields = []
            for field in range(3):
                value = pick(found[0][field], centers[ring])
                if ring:
                    value = jnp.where(p == 0, value, pick(found[1][field], centers[ring]))
                fields.append(value)
            power = pick([8**i for i in range(8)], me[ring])
            fields[:2] = [lax.rem(lax.div(value, power), 8) for value in fields[:2]]
            route.append(fields)

    def inj_hop(ring, e, d, ch, k, to, sem):
        ref = piece(ring, ch, k)
        return copy(
            ref, ref, sem.at[ring, e, d - 1, ch], inj_r.at[ring, e, d - 1, ch],
            dev(r, to, s) if ring == 0 else dev(to, z, s),
        )

    def inject(chs, t):
        for ch in chs:
            for ring in range(2):
                depth, to, second = route[2 * ring + ch % 2]
                d = t - depth
                for e in range(2):
                    k, exists = mirrored(ring, e, d)
                    here = exists & (d >= 1) & (d <= (3 if e else 4))

                    @pl.when(here & (depth > 0))
                    def _():
                        inj_hop(ring, e, d, ch, k, to, inj_s).wait_recv()

                    if t <= 4:

                        @pl.when(here & diag)
                        def _():
                            if ring == 0:
                                rowb[chunk(ch), quarter(k)] = colb[quarter(k), chunk(ch)].T
                            else:
                                colb[quarter(k), chunk(ch)] = rowb[chunk(ch), quarter(k)].T

                    @pl.when(here & (to != me[ring]) & (diag | (depth > 0)))
                    def _():
                        inj_hop(ring, e, d, ch, k, to, inj_s).start()

                    if t <= 4:

                        @pl.when(here & diag & (second != me[ring]))
                        def _():
                            inj_hop(ring, e, d, ch, k, second, inj_l).start()

    def matmul(chs, nq):
        cols = quarter(nq)
        for ch in chs:
            rows = chunk(ch)
            part[rows, cols] = jnp.dot(
                rowb[rows, :], colb[:, cols], preferred_element_type=jnp.float32
            )

    sibling = dev(r, z, 2 * p + (1 - q))
    partner = dev(r, z, 2 * (1 - p) + q)

    def sib_away(ch):
        return copy(
            part.at[chunk(ch), quarter(away + 1 - q)], sibb.at[chunk(ch), pl.ds(0, TILE)],
            sib_s.at[ch], sib_r.at[ch], sibling,
        )

    def sib_home():
        return copy(
            part.at[:, quarter(home + 1 - q)], sibb.at[:, pl.ds(TILE, TILE)],
            sib_s.at[CHUNKS], sib_r.at[CHUNKS], sibling,
        )

    def y_copy(ch):
        rows = chunk(ch)
        return copy(ysend.at[rows, :], yrecv.at[rows, :], y_s.at[ch], y_r.at[ch], partner)

    def y_in(ch):
        rows = chunk((ch + 2) % 4)
        return copy(ysend.at[rows, :], yrecv.at[rows, :], y_s.at[ch], y_r.at[ch], partner)

    def away_1(ch):
        @pl.when(active)
        def _():
            matmul((ch,), away + 1 - q)
            sib_away(ch).start()
            matmul((ch,), away + q)

    def away_2(ch):
        @pl.when(active)
        def _():
            sib_away(ch).wait_recv()
            rows = chunk(ch)
            ysend[rows, :] = part[rows, quarter(away + q)] + sibb[rows, pl.ds(0, TILE)]
            y_copy(ch).start()

    def trq_copy(o):
        return copy(trq.at[s], trq.at[s], trq_s.at[o], trq_r.at[s], dev(r, z, o))

    def trq_in(o):
        return copy(trq.at[o], trq.at[o], trq_s.at[o], trq_r.at[o], dev(r, z, o))

    def total(ref, n):
        value = ref[0]
        for i in range(1, n):
            value = value + ref[i]
        return value

    for o in others:

        @pl.when((r < z) | (diag & (o < s)))
        def _():
            intra(o).start()

    @pl.when(r < z)
    def _():
        rowb[:, quarter(z)] = tbuf[...]
        own(0, (0, 1))
        colb[quarter(r), quarter(s)] = tbuf[quarter(s), :]
        for o in others:
            intra_in(o).wait_recv()

    @pl.when(diag)
    def _():
        block = tbuf[quarter(s), :].astype(jnp.float32)
        above = lax.broadcasted_iota(jnp.int32, block.shape, 0) // BLK
        right = lax.broadcasted_iota(jnp.int32, block.shape, 1) // BLK
        strict = jnp.where(right > above, block, jnp.zeros_like(block))
        whole = (block + strict.T).astype(jnp.bfloat16)
        rowb[quarter(s), quarter(z)] = whole
        colb[quarter(r), quarter(s)] = whole
        for o in others:

            @pl.when(o < s)
            def _():
                rowb[quarter(o), quarter(z)] = tbuf[quarter(o), :]
                colb[quarter(r), quarter(o)] = tbuf[quarter(o), :].T

            @pl.when(o > s)
            def _():
                intra_in(o).wait_recv()
                rowb[quarter(o), quarter(z)] = colb[quarter(r), quarter(o)].T

        own(0, (0, 1))

    own(1, (0, 1))
    tr_own(0)
    end = 4 + DEEPEST
    for u in range(1, end + LAG * (CHUNKS - 1) + 1):
        for ch in range(2, CHUNKS):
            if u == LAG * ch - 1:
                for ring in range(2):
                    own(ring, (ch,))
        for ch in range(CHUNKS):
            if 1 <= u - LAG * ch <= 4:
                natural((ch,), u - LAG * ch)
        for ch in range(CHUNKS):
            if 1 <= u - LAG * ch <= end:
                inject((ch,), u - LAG * ch)
        if u <= 4:
            tr_step(0, u)
        if u == 5:
            tr[1, r] = total(tr.at[0], 8)
            tr_own(1)
        if 6 <= u <= 9:
            tr_step(1, u - 5)
        if u == 10:
            trq[s] = total(tr.at[1], 8)
            for o in others:
                trq_copy(o).start()
        if u == end + LAG:
            away_1(0)
            away_1(1)
        if u == end + LAG + 1:
            away_2(0)
            away_2(1)
        if u == end + 2 * LAG:
            away_1(2)
        if u == end + 2 * LAG + 1:
            away_2(2)
    away_1(3)
    away_2(3)

    @pl.when(active)
    def _():
        matmul(range(CHUNKS), home + 1 - q)
        sib_home().start()
        matmul(range(CHUNKS), home + q)

    for o in others:
        trq_in(o).wait_recv()
    sums = total(trq, 4)
    traces[0] = jnp.sum(sums[0:8, :]) / (NSUP * SUPER)
    traces[1] = jnp.sum(sums[8:16, :]) / (NSUP * SUPER)

    @pl.when(active)
    def _():
        sib_home().wait_recv()
        for ch in range(CHUNKS):
            y_in(ch).wait_recv()
        for i in range(8):
            rows = pl.ds(i * BLK, BLK)
            value = part[rows, quarter(home + q)] + sibb[rows, pl.ds(TILE, TILE)] + yrecv[rows, :]
            for j in range(2):
                kept, _same = keep(i, j)
                block = value[:, j * BLK:(j + 1) * BLK]
                block = jnp.where(kept, block, jnp.zeros_like(block))
                out[rows, pl.ds(j * BLK, BLK)] = block.astype(jnp.bfloat16)

    @pl.when(r > z)
    def _():
        out[...] = jnp.zeros_like(out)

    for ring, d in ringdirs:
        for t in (1, 2, 3, 4):
            k = item_at(ring, d, t - 1)
            if has_hop(d, 0, t):
                tr_hop(ring, d, t, k).wait_send()

            for ch in range(CHUNKS):
                if has_hop(d, ch, t):

                    @pl.when(stored(ring, k) & goes(ring, d, ch, t))
                    def _():
                        hop(ring, d, ch, t, k).wait_send()

    for ch in range(CHUNKS):
        for ring in range(2):
            depth, to, second = route[2 * ring + ch % 2]
            for e in range(2):
                for d in range(1, 4 if e else 5):
                    k, exists = mirrored(ring, e, d)

                    @pl.when(exists & (to != me[ring]) & (diag | (depth > 0)))
                    def _():
                        inj_hop(ring, e, d, ch, k, to, inj_s).wait_send()

                    @pl.when(exists & diag & (second != me[ring]))
                    def _():
                        inj_hop(ring, e, d, ch, k, second, inj_l).wait_send()

    for o in others:
        trq_copy(o).wait_send()

    @pl.when(active)
    def _():
        for ch in range(CHUNKS):
            sib_away(ch).wait_send()
            y_copy(ch).wait_send()
        sib_home().wait_send()

    for o in others:

        @pl.when((r < z) | (diag & (o < s)))
        def _():
            intra(o).wait_send()


def per_device(density, pattern):
    dma = pltpu.SemaphoreType.DMA
    f32, bf16 = jnp.float32, jnp.bfloat16
    return pl.pallas_call(
        kernel,
        out_shape=(
            jax.ShapeDtypeStruct(density.shape, bf16),
            jax.ShapeDtypeStruct((2,), f32),
        ),
        in_specs=[pl.BlockSpec(memory_space=pl.ANY)] * 2,
        out_specs=(
            pl.BlockSpec(memory_space=pltpu.VMEM),
            pl.BlockSpec(memory_space=pltpu.SMEM),
        ),
        scratch_shapes=[
            pltpu.SMEM(pattern.shape, pattern.dtype),
            pltpu.VMEM(density.shape, density.dtype),
            dma((2,)),
            pltpu.VMEM((SUPER, TILE), bf16),
            pltpu.VMEM((SUPER, NSUP * TILE), bf16),
            pltpu.VMEM((NSUP * TILE, SUPER), bf16),
            pltpu.VMEM((SUPER, SUPER), f32),
            pltpu.VMEM((SUPER, 2 * TILE), f32),
            pltpu.VMEM((SUPER, TILE), f32),
            pltpu.VMEM((SUPER, TILE), f32),
            pltpu.VMEM((2, NSUP, 16, BLK), f32),
            pltpu.VMEM((4, 16, BLK), f32),
            dma((2, 2, CHUNKS, 4)), dma((2, 2, CHUNKS, 4)),
            dma((2, 2, 4, CHUNKS)), dma((2, 2, 4, CHUNKS)), dma((2, 2, 4, CHUNKS)),
            dma((2, 2, 4)), dma((2, 2, 4)), dma((4,)), dma((4,)),
            dma((4,)), dma((4,)),
            dma((CHUNKS + 1,)), dma((CHUNKS + 1,)), dma((CHUNKS,)), dma((CHUNKS,)),
        ],
        compiler_params=pltpu.CompilerParams(
            collective_id=0, has_side_effects=True, vmem_limit_bytes=40 * 1024 * 1024
        ),
        cost_estimate=pl.CostEstimate(
            flops=2 * SUPER * SUPER * NSUP * TILE, bytes_accessed=2 * 1024 * 1024, transcendentals=0
        ),
    )(pattern, density)


def solution(mesh):
    return jax.shard_map(
        per_device, mesh=mesh, in_specs=(P("row", "col"), P()),
        out_specs=(P("row", "col"), P()), check_vma=False,
    )
```

```python
import jax
import jax.numpy as jnp
from jax import lax
from jax.experimental import pallas as pl
from jax.experimental.pallas import tpu as pltpu
from jax.sharding import PartitionSpec as P

BLK = 128
MESH = pl.DeviceIdType.MESH
TILE = 256
SUPER = 1024
NSUP = 8
CHUNKS = 4
LAG = 2


def ring_order(r, p):
    x, hi = lax.div(r, 2), lax.rem(r, 2)
    xx = lax.rem(x + 2 * p, 4)
    return xx * (1 - hi) + (7 - xx) * hi


def ring_row(h, p):
    hi = lax.div(h, 4)
    xx = h * (1 - hi) + (7 - h) * hi
    return 2 * lax.rem(xx + 2 * p, 4) + hi


CHAINS = (
    (
        (
            (((), ()), ((), ())),
            (((7, 6, 5,), (2, 3, 4,)), ((7, 6, 5,), (2, 3, 4,))),
            (((3, 4,), (7, 6, 5,)), ((3, 4, 5,), (7, 6,))),
            (((4,), (1, 7, 6, 5,)), ((2, 7, 6,), (4, 5,))),
            (((2, 7, 6, 5,), ()), ((5, 6,), (1, 7,))),
            (((), (2, 7, 6,)), ((6, 7,), ())),
            (((), (7,)), ((), (3, 0, 7,))),
            (((), ()), ((), ())),
        ),
    ),
    (
        (
            (((), ()), ((), ())),
            (((), (4, 0,)), ((), (0,))),
            (((), (3, 1, 0,)), ((0, 7, 1,), ())),
            (((4, 2, 0,), (1,)), ((1,), (2, 0,))),
            (((2, 0,), (3, 1,)), ((5, 3, 1,), (6, 0, 2,))),
            (((4, 2, 0,), (3, 1,)), ((3, 1, 0,), (2, 4,))),
            (((4, 2, 5,), (0, 3, 1,)), ((4, 2, 5,), (0, 1, 3,))),
            (((), ()), ((), ())),
        ),
        (
            (((), ()), ((), ())),
            (((6, 0,), ()), ((), (2, 0,))),
            (((0, 7, 1,), ()), ((4, 6, 0,), (5, 3, 1,))),
            (((5, 7, 1,), (4, 2, 0,)), ((1, 0, 2,), ())),
            (((7, 1, 3,), (6, 0, 2,)), ((5, 3, 1,), (2, 0,))),
            (((4, 2, 0,), (3, 1,)), ((2, 4,), (3, 1, 0,))),
            (((4, 2, 5,), (0, 1, 3,)), ((1, 3, 5,), (4, 2, 0,))),
            (((), ()), ((), ())),
        ),
    ),
)


def chains(ring, p, center, parity):
    table, firsts = {}, []
    for places in CHAINS[ring][p][center][parity]:
        for depth, place in enumerate(places):
            assert place not in table
            following = places[depth + 1] if depth + 1 < len(places) else place
            table[place] = (depth + 1, following)
        firsts.append(places[0] if places else center)
    table[center] = (0, firsts[0])
    return table, firsts[1]


def packed(ring, p, parity):
    depths, nexts, seconds = [], [], []
    for center in range(8):
        table, second = chains(ring, p, center, parity)
        depths.append(sum(table.get(i, (0, i))[0] * 8**i for i in range(8)))
        nexts.append(sum(table.get(i, (0, i))[1] * 8**i for i in range(8)))
        seconds.append(second)
    return depths, nexts, seconds


DEEPEST = max(
    depth
    for ring in range(2)
    for p in range(1 + ring)
    for center in range(8)
    for parity in range(2)
    for depth, _next in chains(ring, p, center, parity)[0].values()
)


def pick(values, index):
    result = jnp.int32(values[0])
    for i, value in enumerate(values):
        result = jnp.where(index == i, jnp.int32(value), result)
    return result


def kernel(
    pat_in, dens_in, out, traces,
    pat, dens, in_sem,
    tbuf, rowb, colb, part, sibb, ysend, yrecv, tr, trq,
    ring_s, ring_r, inj_s, inj_l, inj_r, tr_s, tr_r, trq_s, trq_r,
    intra_s, intra_r, sib_s, sib_r, y_s, y_r,
):
    r = lax.axis_index("row")
    c = lax.axis_index("col")
    z, s = lax.div(c, 4), lax.rem(c, 4)
    p, q = lax.div(s, 2), lax.rem(s, 2)
    active, diag = r <= z, r == z

    def dev(r_, z_, s_):
        return (r_, 4 * z_ + s_)

    def copy(src, dst, ssem, rsem, device):
        return pltpu.make_async_remote_copy(
            src_ref=src, dst_ref=dst, send_sem=ssem, recv_sem=rsem,
            device_id=device, device_id_type=MESH,
        )

    def wrap(i):
        return lax.rem(i + 8, 8)

    h = ring_order(r, p)
    neighbours = (
        (dev(r, wrap(z + 1), s), dev(r, wrap(z - 1), s)),
        (dev(ring_row(wrap(h + 1), p), z, s), dev(ring_row(wrap(h - 1), p), z, s)),
    )
    others = [lax.rem(s + d, 4) for d in (1, 2, 3)]

    barrier = pltpu.get_barrier_semaphore()
    for i in range(1, 8):
        for device in (dev(r, wrap(z + i), s), dev(wrap(r + i), z, s)):
            pl.semaphore_signal(barrier, inc=1, device_id=device, device_id_type=MESH)
    for o in others:
        pl.semaphore_signal(barrier, inc=1, device_id=dev(r, z, o), device_id_type=MESH)

    inputs = (
        pltpu.make_async_copy(pat_in, pat, in_sem.at[0]),
        pltpu.make_async_copy(dens_in, dens, in_sem.at[1]),
    )
    for item in inputs:
        item.start()
    for item in inputs:
        item.wait()

    def keep(i, j):
        bi, bj = r * 8 + i, c * 2 + j
        return ((pat[bi, bj] != 0) | (bi == bj)) & (bj >= bi), bi == bj

    def quarter(i):
        return pl.ds(pl.multiple_of(i * TILE, TILE), TILE)

    eye = lax.broadcasted_iota(jnp.int32, (BLK, BLK), 0) == lax.broadcasted_iota(jnp.int32, (BLK, BLK), 1)
    first = jnp.zeros((BLK, BLK), jnp.float32)
    second = jnp.zeros((BLK, BLK), jnp.float32)
    for i in range(8):
        for j in range(2):
            kept, same = keep(i, j)
            block = dens[pl.ds(i * BLK, BLK), pl.ds(j * BLK, BLK)].astype(jnp.float32)
            block = jnp.where(kept, block, jnp.zeros_like(block))
            tbuf[pl.ds(i * BLK, BLK), pl.ds(j * BLK, BLK)] = block.astype(jnp.bfloat16)
            first = first + jnp.where(eye & same, block, jnp.zeros_like(block))
            square = block * block
            second = second + jnp.where(same, square, square + square)

    tr[0, z, 0:8, :] = first.reshape(BLK // 8, 8, BLK).sum(axis=0)
    tr[0, z, 8:16, :] = second.reshape(BLK // 8, 8, BLK).sum(axis=0)

    pl.semaphore_wait(barrier, 17)

    def intra(o):
        return copy(
            tbuf.at[quarter(o), :], colb.at[quarter(r), quarter(s)],
            intra_s.at[o], intra_r.at[s], dev(r, z, o),
        )

    def intra_in(o):
        return copy(
            tbuf.at[quarter(o), :], colb.at[quarter(r), quarter(o)],
            intra_s.at[o], intra_r.at[o], dev(r, z, o),
        )

    away, home = (1 - p) * 2, p * 2
    pos = (z, h)

    def chunk(ch):
        return quarter((away if ch < 2 else home) + ch % 2)

    def piece(ring, ch, k):
        return rowb.at[chunk(ch), quarter(k)] if ring == 0 else colb.at[quarter(k), chunk(ch)]

    def at(ring, where):
        return wrap(where) if ring == 0 else ring_row(wrap(where), p)

    def item_at(ring, d, dist):
        return at(ring, pos[ring] - dist if d == 0 else pos[ring] + dist)

    def stored(ring, k):
        return k >= r if ring == 0 else k <= z

    def has_hop(d, ch, t):
        return t <= 3 or (t == 4 and ch % 2 == d)

    def hop(ring, d, ch, t, k):
        ref = piece(ring, ch, k)
        return copy(
            ref, ref, ring_s.at[ring, d, ch, t - 1], ring_r.at[ring, d, ch, t - 1],
            neighbours[ring][d],
        )

    ringdirs = [(a, d) for a in range(2) for d in range(2)]

    def tr_hop(ring, d, t, k):
        ref = tr.at[ring, k]
        return copy(ref, ref, tr_s.at[ring, d, t - 1], tr_r.at[ring, d, t - 1], neighbours[ring][d])

    ahead = [
        [
            [r <= wrap(z + i) if d == 0 else r <= wrap(z - i) for i in range(5)],
            [at(1, h + i) <= z if d == 0 else at(1, h - i) <= z for i in range(5)],
        ]
        for d in range(2)
    ]

    def served(ring, d, i, j):
        result = ahead[d][ring][i]
        for k in range(i + 1, j + 1):
            result = result | ahead[d][ring][k]
        return result

    def goes(ring, d, ch, t):
        return served(ring, d, 1, (4 if ch % 2 == d else 3) - t + 1)

    def comes(ring, d, ch, t):
        return served(ring, d, 0, (4 if ch % 2 == d else 3) - t)

    def own(ring, chs):
        for ch in chs:
            for d in range(2):

                @pl.when(active & goes(ring, d, ch, 1))
                def _():
                    hop(ring, d, ch, 1, item_at(ring, d, 0)).start()

    def tr_own(ring):
        for d in range(2):
            tr_hop(ring, d, 1, item_at(ring, d, 0)).start()

    def natural(chs, t):
        for ch in chs:
            for ring, d in ringdirs:
                if not has_hop(d, ch, t):
                    continue
                k = item_at(ring, d, t)

                @pl.when(stored(ring, k) & comes(ring, d, ch, t))
                def _():
                    hop(ring, d, ch, t, k).wait_recv()

                if has_hop(d, ch, t + 1):

                    @pl.when(stored(ring, k) & goes(ring, d, ch, t + 1))
                    def _():
                        hop(ring, d, ch, t + 1, k).start()

    def tr_step(ring, t):
        for d in range(2):
            if has_hop(d, 0, t):
                k = item_at(ring, d, t)
                tr_hop(ring, d, t, k).wait_recv()
                if has_hop(d, 0, t + 1):
                    tr_hop(ring, d, t + 1, k).start()

    def mirrored(ring, e, d):
        source = (ring_order(r, p), z)[ring]
        k = at(1 - ring, source - d if e == 0 else source + d)
        return k, (k < r if ring == 0 else k > z)

    me = (z, r)
    centers = (r, z)
    route = []
    for ring in range(2):
        for parity in range(2):
            found = [packed(ring, i, parity) for i in range(1 + ring)]
            fields = []
            for field in range(3):
                value = pick(found[0][field], centers[ring])
                if ring:
                    value = jnp.where(p == 0, value, pick(found[1][field], centers[ring]))
                fields.append(value)
            power = pick([8**i for i in range(8)], me[ring])
            fields[:2] = [lax.rem(lax.div(value, power), 8) for value in fields[:2]]
            route.append(fields)

    def inj_hop(ring, e, d, ch, k, to, sem):
        ref = piece(ring, ch, k)
        return copy(
            ref, ref, sem.at[ring, e, d - 1, ch], inj_r.at[ring, e, d - 1, ch],
            dev(r, to, s) if ring == 0 else dev(to, z, s),
        )

    def inject(chs, t):
        for ch in chs:
            for ring in range(2):
                depth, to, second = route[2 * ring + ch % 2]
                d = t - depth
                for e in range(2):
                    k, exists = mirrored(ring, e, d)
                    here = exists & (d >= 1) & (d <= (3 if e else 4))

                    @pl.when(here & (depth > 0))
                    def _():
                        inj_hop(ring, e, d, ch, k, to, inj_s).wait_recv()

                    if t <= 4:

                        @pl.when(here & diag)
                        def _():
                            if ring == 0:
                                rowb[chunk(ch), quarter(k)] = colb[quarter(k), chunk(ch)].T
                            else:
                                colb[quarter(k), chunk(ch)] = rowb[chunk(ch), quarter(k)].T

                    @pl.when(here & (to != me[ring]) & (diag | (depth > 0)))
                    def _():
                        inj_hop(ring, e, d, ch, k, to, inj_s).start()

                    if t <= 4:

                        @pl.when(here & diag & (second != me[ring]))
                        def _():
                            inj_hop(ring, e, d, ch, k, second, inj_l).start()

    def matmul(chs, nq):
        cols = quarter(nq)
        for ch in chs:
            rows = chunk(ch)
            part[rows, cols] = jnp.dot(
                rowb[rows, :], colb[:, cols], preferred_element_type=jnp.float32
            )

    sibling = dev(r, z, 2 * p + (1 - q))
    partner = dev(r, z, 2 * (1 - p) + q)

    def sib_away(ch):
        return copy(
            part.at[chunk(ch), quarter(away + 1 - q)], sibb.at[chunk(ch), pl.ds(0, TILE)],
            sib_s.at[ch], sib_r.at[ch], sibling,
        )

    def sib_home():
        return copy(
            part.at[:, quarter(home + 1 - q)], sibb.at[:, pl.ds(TILE, TILE)],
            sib_s.at[CHUNKS], sib_r.at[CHUNKS], sibling,
        )

    def y_copy(ch):
        rows = chunk(ch)
        return copy(ysend.at[rows, :], yrecv.at[rows, :], y_s.at[ch], y_r.at[ch], partner)

    def y_in(ch):
        rows = chunk((ch + 2) % 4)
        return copy(ysend.at[rows, :], yrecv.at[rows, :], y_s.at[ch], y_r.at[ch], partner)

    def away_1(ch):
        @pl.when(active)
        def _():
            matmul((ch,), away + 1 - q)
            sib_away(ch).start()
            matmul((ch,), away + q)

    def away_2(ch):
        @pl.when(active)
        def _():
            sib_away(ch).wait_recv()
            rows = chunk(ch)
            ysend[rows, :] = part[rows, quarter(away + q)] + sibb[rows, pl.ds(0, TILE)]
            y_copy(ch).start()

    def trq_copy(o):
        return copy(trq.at[s], trq.at[s], trq_s.at[o], trq_r.at[s], dev(r, z, o))

    def trq_in(o):
        return copy(trq.at[o], trq.at[o], trq_s.at[o], trq_r.at[o], dev(r, z, o))

    def total(ref, n):
        value = ref[0]
        for i in range(1, n):
            value = value + ref[i]
        return value

    for o in others:

        @pl.when((r < z) | (diag & (o < s)))
        def _():
            intra(o).start()

    @pl.when(r < z)
    def _():
        rowb[:, quarter(z)] = tbuf[...]
        own(0, (0, 1))
        colb[quarter(r), quarter(s)] = tbuf[quarter(s), :]
        for o in others:
            intra_in(o).wait_recv()

    @pl.when(diag)
    def _():
        block = tbuf[quarter(s), :].astype(jnp.float32)
        above = lax.broadcasted_iota(jnp.int32, block.shape, 0) // BLK
        right = lax.broadcasted_iota(jnp.int32, block.shape, 1) // BLK
        strict = jnp.where(right > above, block, jnp.zeros_like(block))
        whole = (block + strict.T).astype(jnp.bfloat16)
        rowb[quarter(s), quarter(z)] = whole
        colb[quarter(r), quarter(s)] = whole
        for o in others:

            @pl.when(o < s)
            def _():
                rowb[quarter(o), quarter(z)] = tbuf[quarter(o), :]
                colb[quarter(r), quarter(o)] = tbuf[quarter(o), :].T

            @pl.when(o > s)
            def _():
                intra_in(o).wait_recv()
                rowb[quarter(o), quarter(z)] = colb[quarter(r), quarter(o)].T

        own(0, (0, 1))

    own(1, (0, 1))
    tr_own(0)
    end = 4 + DEEPEST
    for u in range(1, end + LAG * (CHUNKS - 1) + 1):
        for ch in range(2, CHUNKS):
            if u == LAG * ch - 1:
                for ring in range(2):
                    own(ring, (ch,))
        for ch in range(CHUNKS):
            if 1 <= u - LAG * ch <= 4:
                natural((ch,), u - LAG * ch)
        for ch in range(CHUNKS):
            if 1 <= u - LAG * ch <= end:
                inject((ch,), u - LAG * ch)
        if u <= 4:
            tr_step(0, u)
        if u == 5:
            tr[1, r] = total(tr.at[0], 8)
            tr_own(1)
        if 6 <= u <= 9:
            tr_step(1, u - 5)
        if u == 10:
            trq[s] = total(tr.at[1], 8)
            for o in others:
                trq_copy(o).start()
        if u == end + LAG:
            away_1(0)
            away_1(1)
        if u == end + LAG + 1:
            away_2(0)
            away_2(1)
        if u == end + 2 * LAG:
            away_1(2)
        if u == end + 2 * LAG + 1:
            away_2(2)
    away_1(3)
    away_2(3)

    @pl.when(active)
    def _():
        matmul(range(CHUNKS), home + 1 - q)
        sib_home().start()
        matmul(range(CHUNKS), home + q)

    for o in others:
        trq_in(o).wait_recv()
    sums = total(trq, 4)
    traces[0] = jnp.sum(sums[0:8, :]) / (NSUP * SUPER)
    traces[1] = jnp.sum(sums[8:16, :]) / (NSUP * SUPER)

    @pl.when(active)
    def _():
        sib_home().wait_recv()
        for ch in range(CHUNKS):
            y_in(ch).wait_recv()
        for i in range(8):
            rows = pl.ds(i * BLK, BLK)
            value = part[rows, quarter(home + q)] + sibb[rows, pl.ds(TILE, TILE)] + yrecv[rows, :]
            for j in range(2):
                kept, _same = keep(i, j)
                block = value[:, j * BLK:(j + 1) * BLK]
                block = jnp.where(kept, block, jnp.zeros_like(block))
                out[rows, pl.ds(j * BLK, BLK)] = block.astype(jnp.bfloat16)

    @pl.when(r > z)
    def _():
        out[...] = jnp.zeros_like(out)

    for ring, d in ringdirs:
        for t in (1, 2, 3, 4):
            k = item_at(ring, d, t - 1)
            if has_hop(d, 0, t):
                tr_hop(ring, d, t, k).wait_send()

            for ch in range(CHUNKS):
                if has_hop(d, ch, t):

                    @pl.when(stored(ring, k) & goes(ring, d, ch, t))
                    def _():
                        hop(ring, d, ch, t, k).wait_send()

    for ch in range(CHUNKS):
        for ring in range(2):
            depth, to, second = route[2 * ring + ch % 2]
            for e in range(2):
                for d in range(1, 4 if e else 5):
                    k, exists = mirrored(ring, e, d)

                    @pl.when(exists & (to != me[ring]) & (diag | (depth > 0)))
                    def _():
                        inj_hop(ring, e, d, ch, k, to, inj_s).wait_send()

                    @pl.when(exists & diag & (second != me[ring]))
                    def _():
                        inj_hop(ring, e, d, ch, k, second, inj_l).wait_send()

    for o in others:
        trq_copy(o).wait_send()

    @pl.when(active)
    def _():
        for ch in range(CHUNKS):
            sib_away(ch).wait_send()
            y_copy(ch).wait_send()
        sib_home().wait_send()

    for o in others:

        @pl.when((r < z) | (diag & (o < s)))
        def _():
            intra(o).wait_send()


def per_device(density, pattern):
    dma = pltpu.SemaphoreType.DMA
    f32, bf16 = jnp.float32, jnp.bfloat16
    return pl.pallas_call(
        kernel,
        out_shape=(
            jax.ShapeDtypeStruct(density.shape, bf16),
            jax.ShapeDtypeStruct((2,), f32),
        ),
        in_specs=[pl.BlockSpec(memory_space=pl.ANY)] * 2,
        out_specs=(
            pl.BlockSpec(memory_space=pltpu.VMEM),
            pl.BlockSpec(memory_space=pltpu.SMEM),
        ),
        scratch_shapes=[
            pltpu.SMEM(pattern.shape, pattern.dtype),
            pltpu.VMEM(density.shape, density.dtype),
            dma((2,)),
            pltpu.VMEM((SUPER, TILE), bf16),
            pltpu.VMEM((SUPER, NSUP * TILE), bf16),
            pltpu.VMEM((NSUP * TILE, SUPER), bf16),
            pltpu.VMEM((SUPER, SUPER), f32),
            pltpu.VMEM((SUPER, 2 * TILE), f32),
            pltpu.VMEM((SUPER, TILE), f32),
            pltpu.VMEM((SUPER, TILE), f32),
            pltpu.VMEM((2, NSUP, 16, BLK), f32),
            pltpu.VMEM((4, 16, BLK), f32),
            dma((2, 2, CHUNKS, 4)), dma((2, 2, CHUNKS, 4)),
            dma((2, 2, 4, CHUNKS)), dma((2, 2, 4, CHUNKS)), dma((2, 2, 4, CHUNKS)),
            dma((2, 2, 4)), dma((2, 2, 4)), dma((4,)), dma((4,)),
            dma((4,)), dma((4,)),
            dma((CHUNKS + 1,)), dma((CHUNKS + 1,)), dma((CHUNKS,)), dma((CHUNKS,)),
        ],
        compiler_params=pltpu.CompilerParams(
            collective_id=0, has_side_effects=True, vmem_limit_bytes=62 * 1024 * 1024
        ),
        cost_estimate=pl.CostEstimate(
            flops=2 * SUPER * SUPER * NSUP * TILE, bytes_accessed=2 * 1024 * 1024, transcendentals=0
        ),
    )(pattern, density)


def solution(mesh):
    return jax.shard_map(
        per_device, mesh=mesh, in_specs=(P("row", "col"), P()),
        out_specs=(P("row", "col"), P()), check_vma=False,
    )
```

```python
import jax
import jax.numpy as jnp
from jax import lax
from jax.experimental import pallas as pl
from jax.experimental.pallas import tpu as pltpu
from jax.sharding import PartitionSpec as P

BLK = 128
MESH = pl.DeviceIdType.MESH
TILE = 256
SUPER = 1024
NSUP = 8
CHUNKS = 4
LAG = 2


def ring_order(r, p):
    x, hi = lax.div(r, 2), lax.rem(r, 2)
    xx = lax.rem(x + 2 * p, 4)
    return xx * (1 - hi) + (7 - xx) * hi


def ring_row(h, p):
    hi = lax.div(h, 4)
    xx = h * (1 - hi) + (7 - h) * hi
    return 2 * lax.rem(xx + 2 * p, 4) + hi


CHAINS = (
    (
        (
            (((), ()), ((), ())),
            (((7, 6, 5,), (2, 3, 4,)), ((7, 6, 5,), (2, 3, 4,))),
            (((3, 4,), (7, 6, 5,)), ((3, 4, 5,), (7, 6,))),
            (((4,), (1, 7, 6, 5,)), ((2, 7, 6,), (4, 5,))),
            (((2, 7, 6, 5,), ()), ((5, 6,), (1, 7,))),
            (((), (2, 7, 6,)), ((6, 7,), ())),
            (((), (7,)), ((), (3, 0, 7,))),
            (((), ()), ((), ())),
        ),
    ),
    (
        (
            (((), ()), ((), ())),
            (((), (4, 0,)), ((), (0,))),
            (((), (3, 1, 0,)), ((0, 7, 1,), ())),
            (((4, 2, 0,), (1,)), ((1,), (2, 0,))),
            (((2, 0,), (3, 1,)), ((5, 3, 1,), (6, 0, 2,))),
            (((4, 2, 0,), (3, 1,)), ((3, 1, 0,), (2, 4,))),
            (((4, 2, 5,), (0, 3, 1,)), ((4, 2, 5,), (0, 1, 3,))),
            (((), ()), ((), ())),
        ),
        (
            (((), ()), ((), ())),
            (((6, 0,), ()), ((), (2, 0,))),
            (((0, 7, 1,), ()), ((4, 6, 0,), (5, 3, 1,))),
            (((5, 7, 1,), (4, 2, 0,)), ((1, 0, 2,), ())),
            (((7, 1, 3,), (6, 0, 2,)), ((5, 3, 1,), (2, 0,))),
            (((4, 2, 0,), (3, 1,)), ((2, 4,), (3, 1, 0,))),
            (((4, 2, 5,), (0, 1, 3,)), ((1, 3, 5,), (4, 2, 0,))),
            (((), ()), ((), ())),
        ),
    ),
)


def plain_order(p):
    rows = []
    for h in range(8):
        hi = h // 4
        xx = 7 - h if hi else h
        rows.append(2 * ((xx + 2 * p) % 4) + hi)
    return rows


def chains(ring, p, center, parity):
    table, firsts = {}, []
    for places in CHAINS[ring][p][center][parity]:
        for depth, place in enumerate(places):
            assert place not in table
            following = places[depth + 1] if depth + 1 < len(places) else place
            table[place] = (depth + 1, following)
        firsts.append(places[0] if places else center)
    table[center] = (0, firsts[0])
    return table, firsts[1]


def packed(ring, p, parity):
    depths, nexts, seconds = [], [], []
    for center in range(8):
        table, second = chains(ring, p, center, parity)
        depths.append(sum(table.get(i, (0, i))[0] * 8**i for i in range(8)))
        nexts.append(sum(table.get(i, (0, i))[1] * 8**i for i in range(8)))
        seconds.append(second)
    return depths, nexts, seconds


def partners(ring, p):
    order = plain_order(p) if ring else list(range(8))
    masks = []
    for center in range(8):
        pairs = [(order[i], order[(i + 1) % 8]) for i in range(8)]
        for parity in range(2):
            table, second = chains(ring, p, center, parity)
            pairs += [(i, following) for i, (_depth, following) in table.items()] + [(center, second)]
        for me in range(8):
            near = {b for a, b in pairs if a == me} | {a for a, b in pairs if b == me}
            masks.append(sum(2**i for i in near - {me}))
    return masks


DEEPEST = max(
    depth
    for ring in range(2)
    for p in range(1 + ring)
    for center in range(8)
    for parity in range(2)
    for depth, _next in chains(ring, p, center, parity)[0].values()
)


def pick(values, index):
    result = jnp.int32(values[0])
    for i, value in enumerate(values):
        result = jnp.where(index == i, jnp.int32(value), result)
    return result


def kernel(
    pat_in, dens_in, out, traces,
    pat, dens, in_sem,
    tbuf, rowb, colb, part, sibb, ysend, yrecv, tr, trq,
    ring_s, ring_r, inj_s, inj_l, inj_r, tr_s, tr_r, trq_s, trq_r,
    intra_s, intra_r, sib_s, sib_r, y_s, y_r,
):
    r = lax.axis_index("row")
    c = lax.axis_index("col")
    z, s = lax.div(c, 4), lax.rem(c, 4)
    p, q = lax.div(s, 2), lax.rem(s, 2)
    active, diag = r <= z, r == z

    def dev(r_, z_, s_):
        return (r_, 4 * z_ + s_)

    def copy(src, dst, ssem, rsem, device):
        return pltpu.make_async_remote_copy(
            src_ref=src, dst_ref=dst, send_sem=ssem, recv_sem=rsem,
            device_id=device, device_id_type=MESH,
        )

    def wrap(i):
        return lax.rem(i + 8, 8)

    h = ring_order(r, p)
    neighbours = (
        (dev(r, wrap(z + 1), s), dev(r, wrap(z - 1), s)),
        (dev(ring_row(wrap(h + 1), p), z, s), dev(ring_row(wrap(h - 1), p), z, s)),
    )
    others = [lax.rem(s + d, 4) for d in (1, 2, 3)]

    barrier = pltpu.get_barrier_semaphore()
    greeted = jnp.int32(3)
    masks = (
        pick(partners(0, 0), r * 8 + z),
        jnp.where(p == 0, pick(partners(1, 0), z * 8 + r), pick(partners(1, 1), z * 8 + r)),
    )
    for ring in range(2):
        for i in range(8):
            near = lax.rem(lax.div(masks[ring], 2**i), 2)
            greeted = greeted + near

            @pl.when(near == 1)
            def _():
                device = dev(r, i, s) if ring == 0 else dev(i, z, s)
                pl.semaphore_signal(barrier, inc=1, device_id=device, device_id_type=MESH)

    for o in others:
        pl.semaphore_signal(barrier, inc=1, device_id=dev(r, z, o), device_id_type=MESH)

    inputs = (
        pltpu.make_async_copy(pat_in, pat, in_sem.at[0]),
        pltpu.make_async_copy(dens_in, dens, in_sem.at[1]),
    )
    for item in inputs:
        item.start()
    for item in inputs:
        item.wait()

    def keep(i, j):
        bi, bj = r * 8 + i, c * 2 + j
        return ((pat[bi, bj] != 0) | (bi == bj)) & (bj >= bi), bi == bj

    def quarter(i):
        return pl.ds(pl.multiple_of(i * TILE, TILE), TILE)

    eye = lax.broadcasted_iota(jnp.int32, (BLK, BLK), 0) == lax.broadcasted_iota(jnp.int32, (BLK, BLK), 1)
    first = jnp.zeros((BLK, BLK), jnp.float32)
    second = jnp.zeros((BLK, BLK), jnp.float32)
    for i in range(8):
        for j in range(2):
            kept, same = keep(i, j)
            block = dens[pl.ds(i * BLK, BLK), pl.ds(j * BLK, BLK)].astype(jnp.float32)
            block = jnp.where(kept, block, jnp.zeros_like(block))
            tbuf[pl.ds(i * BLK, BLK), pl.ds(j * BLK, BLK)] = block.astype(jnp.bfloat16)
            first = first + jnp.where(eye & same, block, jnp.zeros_like(block))
            square = block * block
            second = second + jnp.where(same, square, square + square)

    tr[0, z, 0:8, :] = first.reshape(BLK // 8, 8, BLK).sum(axis=0)
    tr[0, z, 8:16, :] = second.reshape(BLK // 8, 8, BLK).sum(axis=0)

    pl.semaphore_wait(barrier, greeted)

    def intra(o):
        return copy(
            tbuf.at[quarter(o), :], colb.at[quarter(r), quarter(s)],
            intra_s.at[o], intra_r.at[s], dev(r, z, o),
        )

    def intra_in(o):
        return copy(
            tbuf.at[quarter(o), :], colb.at[quarter(r), quarter(o)],
            intra_s.at[o], intra_r.at[o], dev(r, z, o),
        )

    away, home = (1 - p) * 2, p * 2
    pos = (z, h)

    def chunk(ch):
        return quarter((away if ch < 2 else home) + ch % 2)

    def piece(ring, ch, k):
        return rowb.at[chunk(ch), quarter(k)] if ring == 0 else colb.at[quarter(k), chunk(ch)]

    def at(ring, where):
        return wrap(where) if ring == 0 else ring_row(wrap(where), p)

    def item_at(ring, d, dist):
        return at(ring, pos[ring] - dist if d == 0 else pos[ring] + dist)

    def stored(ring, k):
        return k >= r if ring == 0 else k <= z

    def has_hop(d, ch, t):
        return t <= 3 or (t == 4 and ch % 2 == d)

    def hop(ring, d, ch, t, k):
        ref = piece(ring, ch, k)
        return copy(
            ref, ref, ring_s.at[ring, d, ch, t - 1], ring_r.at[ring, d, ch, t - 1],
            neighbours[ring][d],
        )

    ringdirs = [(a, d) for a in range(2) for d in range(2)]

    def tr_hop(ring, d, t, k):
        ref = tr.at[ring, k]
        return copy(ref, ref, tr_s.at[ring, d, t - 1], tr_r.at[ring, d, t - 1], neighbours[ring][d])

    ahead = [
        [
            [r <= wrap(z + i) if d == 0 else r <= wrap(z - i) for i in range(5)],
            [at(1, h + i) <= z if d == 0 else at(1, h - i) <= z for i in range(5)],
        ]
        for d in range(2)
    ]

    def served(ring, d, i, j):
        result = ahead[d][ring][i]
        for k in range(i + 1, j + 1):
            result = result | ahead[d][ring][k]
        return result

    def goes(ring, d, ch, t):
        return served(ring, d, 1, (4 if ch % 2 == d else 3) - t + 1)

    def comes(ring, d, ch, t):
        return served(ring, d, 0, (4 if ch % 2 == d else 3) - t)

    def own(ring, chs):
        for ch in chs:
            for d in range(2):

                @pl.when(active & goes(ring, d, ch, 1))
                def _():
                    hop(ring, d, ch, 1, item_at(ring, d, 0)).start()

    def tr_own(ring):
        for d in range(2):
            tr_hop(ring, d, 1, item_at(ring, d, 0)).start()

    def natural(chs, t):
        for ch in chs:
            for ring, d in ringdirs:
                if not has_hop(d, ch, t):
                    continue
                k = item_at(ring, d, t)

                @pl.when(stored(ring, k) & comes(ring, d, ch, t))
                def _():
                    hop(ring, d, ch, t, k).wait_recv()

                if has_hop(d, ch, t + 1):

                    @pl.when(stored(ring, k) & goes(ring, d, ch, t + 1))
                    def _():
                        hop(ring, d, ch, t + 1, k).start()

    def tr_step(ring, t):
        for d in range(2):
            if has_hop(d, 0, t):
                k = item_at(ring, d, t)
                tr_hop(ring, d, t, k).wait_recv()
                if has_hop(d, 0, t + 1):
                    tr_hop(ring, d, t + 1, k).start()

    def mirrored(ring, e, d):
        source = (ring_order(r, p), z)[ring]
        k = at(1 - ring, source - d if e == 0 else source + d)
        return k, (k < r if ring == 0 else k > z)

    me = (z, r)
    centers = (r, z)
    route = []
    for ring in range(2):
        for parity in range(2):
            found = [packed(ring, i, parity) for i in range(1 + ring)]
            fields = []
            for field in range(3):
                value = pick(found[0][field], centers[ring])
                if ring:
                    value = jnp.where(p == 0, value, pick(found[1][field], centers[ring]))
                fields.append(value)
            power = pick([8**i for i in range(8)], me[ring])
            fields[:2] = [lax.rem(lax.div(value, power), 8) for value in fields[:2]]
            route.append(fields)

    def inj_hop(ring, e, d, ch, k, to, sem):
        ref = piece(ring, ch, k)
        return copy(
            ref, ref, sem.at[ring, e, d - 1, ch], inj_r.at[ring, e, d - 1, ch],
            dev(r, to, s) if ring == 0 else dev(to, z, s),
        )

    def inject(chs, t):
        for ch in chs:
            for ring in range(2):
                depth, to, second = route[2 * ring + ch % 2]
                d = t - depth
                for e in range(2):
                    k, exists = mirrored(ring, e, d)
                    here = exists & (d >= 1) & (d <= (3 if e else 4))

                    @pl.when(here & (depth > 0))
                    def _():
                        inj_hop(ring, e, d, ch, k, to, inj_s).wait_recv()

                    if t <= 4:

                        @pl.when(here & diag)
                        def _():
                            if ring == 0:
                                rowb[chunk(ch), quarter(k)] = colb[quarter(k), chunk(ch)].T
                            else:
                                colb[quarter(k), chunk(ch)] = rowb[chunk(ch), quarter(k)].T

                    @pl.when(here & (to != me[ring]) & (diag | (depth > 0)))
                    def _():
                        inj_hop(ring, e, d, ch, k, to, inj_s).start()

                    if t <= 4:

                        @pl.when(here & diag & (second != me[ring]))
                        def _():
                            inj_hop(ring, e, d, ch, k, second, inj_l).start()

    def matmul(chs, nq):
        cols = quarter(nq)
        for ch in chs:
            rows = chunk(ch)
            part[rows, cols] = jnp.dot(
                rowb[rows, :], colb[:, cols], preferred_element_type=jnp.float32
            )

    sibling = dev(r, z, 2 * p + (1 - q))
    partner = dev(r, z, 2 * (1 - p) + q)

    def sib_away(ch):
        return copy(
            part.at[chunk(ch), quarter(away + 1 - q)], sibb.at[chunk(ch), pl.ds(0, TILE)],
            sib_s.at[ch], sib_r.at[ch], sibling,
        )

    def sib_home():
        return copy(
            part.at[:, quarter(home + 1 - q)], sibb.at[:, pl.ds(TILE, TILE)],
            sib_s.at[CHUNKS], sib_r.at[CHUNKS], sibling,
        )

    def y_copy(ch):
        rows = chunk(ch)
        return copy(ysend.at[rows, :], yrecv.at[rows, :], y_s.at[ch], y_r.at[ch], partner)

    def y_in(ch):
        rows = chunk((ch + 2) % 4)
        return copy(ysend.at[rows, :], yrecv.at[rows, :], y_s.at[ch], y_r.at[ch], partner)

    def away_1(ch):
        @pl.when(active)
        def _():
            matmul((ch,), away + 1 - q)
            sib_away(ch).start()
            matmul((ch,), away + q)

    def away_2(ch):
        @pl.when(active)
        def _():
            sib_away(ch).wait_recv()
            rows = chunk(ch)
            ysend[rows, :] = part[rows, quarter(away + q)] + sibb[rows, pl.ds(0, TILE)]
            y_copy(ch).start()

    def trq_copy(o):
        return copy(trq.at[s], trq.at[s], trq_s.at[o], trq_r.at[s], dev(r, z, o))

    def trq_in(o):
        return copy(trq.at[o], trq.at[o], trq_s.at[o], trq_r.at[o], dev(r, z, o))

    def total(ref, n):
        value = ref[0]
        for i in range(1, n):
            value = value + ref[i]
        return value

    for o in others:

        @pl.when((r < z) | (diag & (o < s)))
        def _():
            intra(o).start()

    @pl.when(r < z)
    def _():
        rowb[:, quarter(z)] = tbuf[...]
        own(0, (0, 1))
        colb[quarter(r), quarter(s)] = tbuf[quarter(s), :]
        for o in others:
            intra_in(o).wait_recv()

    @pl.when(diag)
    def _():
        block = tbuf[quarter(s), :].astype(jnp.float32)
        above = lax.broadcasted_iota(jnp.int32, block.shape, 0) // BLK
        right = lax.broadcasted_iota(jnp.int32, block.shape, 1) // BLK
        strict = jnp.where(right > above, block, jnp.zeros_like(block))
        whole = (block + strict.T).astype(jnp.bfloat16)
        rowb[quarter(s), quarter(z)] = whole
        colb[quarter(r), quarter(s)] = whole
        for o in others:

            @pl.when(o < s)
            def _():
                rowb[quarter(o), quarter(z)] = tbuf[quarter(o), :]
                colb[quarter(r), quarter(o)] = tbuf[quarter(o), :].T

            @pl.when(o > s)
            def _():
                intra_in(o).wait_recv()
                rowb[quarter(o), quarter(z)] = colb[quarter(r), quarter(o)].T

        own(0, (0, 1))

    own(1, (0, 1))
    tr_own(0)
    end = 4 + DEEPEST
    for u in range(1, end + LAG * (CHUNKS - 1) + 1):
        for ch in range(2, CHUNKS):
            if u == LAG * ch - 1:
                for ring in range(2):
                    own(ring, (ch,))
        for ch in range(CHUNKS):
            if 1 <= u - LAG * ch <= 4:
                natural((ch,), u - LAG * ch)
        for ch in range(CHUNKS):
            if 1 <= u - LAG * ch <= end:
                inject((ch,), u - LAG * ch)
        if u <= 4:
            tr_step(0, u)
        if u == 5:
            tr[1, r] = total(tr.at[0], 8)
            tr_own(1)
        if 6 <= u <= 9:
            tr_step(1, u - 5)
        if u == 10:
            trq[s] = total(tr.at[1], 8)
            for o in others:
                trq_copy(o).start()
        if u == end + LAG:
            away_1(0)
            away_1(1)
        if u == end + LAG + 1:
            away_2(0)
            away_2(1)
        if u == end + 2 * LAG:
            away_1(2)
        if u == end + 2 * LAG + 1:
            away_2(2)
    away_1(3)
    away_2(3)

    @pl.when(active)
    def _():
        matmul(range(CHUNKS), home + 1 - q)
        sib_home().start()
        matmul(range(CHUNKS), home + q)

    for o in others:
        trq_in(o).wait_recv()
    sums = total(trq, 4)
    traces[0] = jnp.sum(sums[0:8, :]) / (NSUP * SUPER)
    traces[1] = jnp.sum(sums[8:16, :]) / (NSUP * SUPER)

    @pl.when(active)
    def _():
        sib_home().wait_recv()
        for ch in range(CHUNKS):
            y_in(ch).wait_recv()
        for i in range(8):
            rows = pl.ds(i * BLK, BLK)
            value = part[rows, quarter(home + q)] + sibb[rows, pl.ds(TILE, TILE)] + yrecv[rows, :]
            for j in range(2):
                kept, _same = keep(i, j)
                block = value[:, j * BLK:(j + 1) * BLK]
                block = jnp.where(kept, block, jnp.zeros_like(block))
                out[rows, pl.ds(j * BLK, BLK)] = block.astype(jnp.bfloat16)

    @pl.when(r > z)
    def _():
        out[...] = jnp.zeros_like(out)

    for ring, d in ringdirs:
        for t in (1, 2, 3, 4):
            k = item_at(ring, d, t - 1)
            if has_hop(d, 0, t):
                tr_hop(ring, d, t, k).wait_send()

            for ch in range(CHUNKS):
                if has_hop(d, ch, t):

                    @pl.when(stored(ring, k) & goes(ring, d, ch, t))
                    def _():
                        hop(ring, d, ch, t, k).wait_send()

    for ch in range(CHUNKS):
        for ring in range(2):
            depth, to, second = route[2 * ring + ch % 2]
            for e in range(2):
                for d in range(1, 4 if e else 5):
                    k, exists = mirrored(ring, e, d)

                    @pl.when(exists & (to != me[ring]) & (diag | (depth > 0)))
                    def _():
                        inj_hop(ring, e, d, ch, k, to, inj_s).wait_send()

                    @pl.when(exists & diag & (second != me[ring]))
                    def _():
                        inj_hop(ring, e, d, ch, k, second, inj_l).wait_send()

    for o in others:
        trq_copy(o).wait_send()

    @pl.when(active)
    def _():
        for ch in range(CHUNKS):
            sib_away(ch).wait_send()
            y_copy(ch).wait_send()
        sib_home().wait_send()

    for o in others:

        @pl.when((r < z) | (diag & (o < s)))
        def _():
            intra(o).wait_send()


def per_device(density, pattern):
    dma = pltpu.SemaphoreType.DMA
    f32, bf16 = jnp.float32, jnp.bfloat16
    return pl.pallas_call(
        kernel,
        out_shape=(
            jax.ShapeDtypeStruct(density.shape, bf16),
            jax.ShapeDtypeStruct((2,), f32),
        ),
        in_specs=[pl.BlockSpec(memory_space=pl.ANY)] * 2,
        out_specs=(
            pl.BlockSpec(memory_space=pltpu.VMEM),
            pl.BlockSpec(memory_space=pltpu.SMEM),
        ),
        scratch_shapes=[
            pltpu.SMEM(pattern.shape, pattern.dtype),
            pltpu.VMEM(density.shape, density.dtype),
            dma((2,)),
            pltpu.VMEM((SUPER, TILE), bf16),
            pltpu.VMEM((SUPER, NSUP * TILE), bf16),
            pltpu.VMEM((NSUP * TILE, SUPER), bf16),
            pltpu.VMEM((SUPER, SUPER), f32),
            pltpu.VMEM((SUPER, 2 * TILE), f32),
            pltpu.VMEM((SUPER, TILE), f32),
            pltpu.VMEM((SUPER, TILE), f32),
            pltpu.VMEM((2, NSUP, 16, BLK), f32),
            pltpu.VMEM((4, 16, BLK), f32),
            dma((2, 2, CHUNKS, 4)), dma((2, 2, CHUNKS, 4)),
            dma((2, 2, 4, CHUNKS)), dma((2, 2, 4, CHUNKS)), dma((2, 2, 4, CHUNKS)),
            dma((2, 2, 4)), dma((2, 2, 4)), dma((4,)), dma((4,)),
            dma((4,)), dma((4,)),
            dma((CHUNKS + 1,)), dma((CHUNKS + 1,)), dma((CHUNKS,)), dma((CHUNKS,)),
        ],
        compiler_params=pltpu.CompilerParams(
            collective_id=0, has_side_effects=True, vmem_limit_bytes=62 * 1024 * 1024
        ),
        cost_estimate=pl.CostEstimate(
            flops=2 * SUPER * SUPER * NSUP * TILE, bytes_accessed=2 * 1024 * 1024, transcendentals=0
        ),
    )(pattern, density)


def solution(mesh):
    return jax.shard_map(
        per_device, mesh=mesh, in_specs=(P("row", "col"), P()),
        out_specs=(P("row", "col"), P()), check_vma=False,
    )
```
